32 devices in a mesh: slab: 2 (over y), gx: 4 (over x, core), gy: 4 (over z).
Axes of the slice: x: 2, y: 2, z: 4, core: 2. Of those that a mesh axis runs over, the one named last changes fastest.
Arguments:
- slab_feature_entries: bfloat16 [64, 32, 8, 512], P(('slab', 'gx'), 'gy'), parts along dimension 0, may hold values from -6 to 6
- depthwise_filter_coefficients: float32 [27, 512], replicated, may hold values from -1.2 to 1.2
- rootmean_scaling_factors: float32 [512], replicated, may hold values from 0.5 to 1.5
- asking_projection_factors: bfloat16 [512, 512], replicated, may hold values from -0.25 to 0.25
- lookup_projection_factors: bfloat16 [512, 512], replicated, may hold values from -0.25 to 0.25
- content_projection_factors: bfloat16 [512, 512], replicated, may hold values from -0.25 to 0.25
- final_projection_factors: bfloat16 [512, 512], replicated, may hold values from -0.25 to 0.25
- softness_per_attender: float32 [8], replicated, may hold values from 4 to 16
- adjacent_block_codes: int32 [16, 8, 2, 7], P(('slab', 'gx'), 'gy'), parts along dimension 0, may hold values from 0 to 6, as said below
- filled_list_lengths: int32 [16, 8, 2], P(('slab', 'gx'), 'gy'), parts along dimension 0, may hold values from 1 to 7, as said below
Outputs:
- mixed: bfloat16 [64, 32, 8, 512], P(('slab', 'gx'), 'gy'), parts along dimension 0
The draws below stay inside these ranges and needn't reach their ends.
There are 2 independent parts, one for each index of `slab`. The reference program is written for one: setup_inputs(seed, part) draws one part's arguments, and reference() takes and returns one part's arrays. A program takes and returns all parts, laid end to end along the dimension named above; an argument that names none is the same for every part. Nothing has to cross between parts.
Inputs may be any that keep to these rules, and one draw needn't show every extreme that they name: `adjacent_block_codes`: every list starts with 0 and holds 7 distinct codes; entries past filled_list_lengths are present but unused. `filled_list_lengths`: some block of every slab uses all 7 entries and some block uses only the first.
All inputs are finite; a program needn't handle non-finite values.
Results may differ from the reference program's by a relative error of at most 0.0075.
Values may be sent and summed in bfloat16 or wider, within the bound.
A program may use at most 128 MiB of HBM per device.

```python
import math
import jax
import jax.numpy as jnp
from jax import lax

D = 512
ATTENDER_COUNT = 8
HD = 64
BLOCK = 4
SLOTS = 7
TZ = 8
NX = 32
NY = 32
BX = 8
BY = 8
BZ = 2


def draw_adjacent_block_codes(key, part):
    total = BX * BY * BZ
    affinity_raw_values = jax.random.randint(jax.random.fold_in(key, 5), (total, 6), 0, 1 << 20) * 8
    affinity_raw_values = affinity_raw_values + jnp.arange(6, dtype=jnp.int32)[None, :]
    order = jnp.argsort(affinity_raw_values, axis=1).astype(jnp.int32) + 1
    lists = jnp.concatenate([jnp.zeros((total, 1), jnp.int32), order], axis=1)
    return lists.reshape(BX, BY, BZ, 7)


def draw_filled_list_lengths(key, part):
    total = BX * BY * BZ
    first, second = jax.random.split(jax.random.fold_in(key, 11), 2)
    values = jax.random.randint(first, (total,), 1, 8).astype(jnp.int32)
    spots = jax.random.permutation(second, total)
    values = values.at[spots[0]].set(7).at[spots[1]].set(1)
    return values.reshape(BX, BY, BZ)


def level_of(rng, shape, shards, low, top_value):
    factor_of, own = 1.0, jax.random.fold_in(rng, 6)
    for axis_at, parts in shards:
        heights = jnp.exp(jax.random.uniform(jax.random.fold_in(own, axis_at), (parts,), jnp.float32, low / len(shards), top_value / len(shards)))
        factor_of = factor_of * jnp.repeat(heights, shape[axis_at] // parts).reshape([-1 if axis == axis_at else 1 for axis in range(len(shape))])
    return factor_of


def normal_values(own_key, extent, spread, most, pieces=(), held_as=jnp.bfloat16):
    values = spread * jax.random.normal(own_key, extent, jnp.float32)
    if pieces:
        values = values * level_of(own_key, extent, pieces, -0.22, 0.18)
    return jnp.clip(values, -most, most).astype(held_as)


def setup_inputs(seed: int = 0, part: int = 0) -> dict:
    streams_of = jax.random.split(jax.random.key(seed), 11)
    part_splits = jax.random.split(jax.random.fold_in(streams_of[10], part), 11)
    return {
        "slab_feature_entries": normal_values(part_splits[0], (NX, NY, TZ, D), 1.0, 6.0, ((0, 4), (1, 4))),
        "depthwise_filter_coefficients": normal_values(streams_of[1], (27, D), 0.2, 1.2, (), jnp.float32),
        "rootmean_scaling_factors": jnp.clip(1.0 + 0.1 * jax.random.normal(streams_of[2], (D,), jnp.float32), 0.5, 1.5),
        "asking_projection_factors": normal_values(streams_of[3], (D, D), D ** -0.5, 0.25),
        "lookup_projection_factors": normal_values(streams_of[4], (D, D), D ** -0.5, 0.25),
        "content_projection_factors": normal_values(streams_of[5], (D, D), D ** -0.5, 0.25),
        "final_projection_factors": normal_values(streams_of[6], (D, D), D ** -0.5, 0.25),
        "softness_per_attender": jnp.clip(jnp.exp(jax.random.uniform(streams_of[7], (ATTENDER_COUNT,), jnp.float32, math.log(4.0), math.log(16.0))), 4.0, 16.0),
        "adjacent_block_codes": draw_adjacent_block_codes(jax.random.fold_in(jax.random.fold_in(streams_of[10], part), 71), part),
        "filled_list_lengths": draw_filled_list_lengths(jax.random.fold_in(jax.random.fold_in(streams_of[10], part), 71), part),
    }


OFFSETS = ((0, 0, 0), (1, 0, 0), (-1, 0, 0), (0, 1, 0), (0, -1, 0), (0, 0, 1), (0, 0, -1))

def conv_sum(padded, depthwise_filter_coefficients, size_x, size_y, size_z):
    summed = padded[1:1 + size_x, 1:1 + size_y, 1:1 + size_z].astype(jnp.float32)
    for tap_index in range(27):
        shift_x = tap_index // 9
        shift_y = tap_index // 3 % 3
        shift_z = tap_index % 3
        piece = padded[shift_x:shift_x + size_x, shift_y:shift_y + size_y, shift_z:shift_z + size_z]
        summed = summed + piece.astype(jnp.float32) * depthwise_filter_coefficients[tap_index]
    return summed.astype(jnp.bfloat16)

def rms_norm(hidden, rootmean_scaling_factors):
    values = hidden.astype(jnp.float32)
    scale = lax.rsqrt(lax.optimization_barrier(jnp.mean(values * values, axis=-1, keepdims=True)) + 1e-05)
    return (values * scale * rootmean_scaling_factors).astype(jnp.bfloat16)

def project(normed, weight_matrix):
    array_extent = normed.shape
    flat = normed.reshape(-1, array_extent[-1])
    result = jnp.dot(flat, weight_matrix, preferred_element_type=jnp.float32).astype(jnp.bfloat16)
    return result.reshape(array_extent[:-1] + (weight_matrix.shape[1],))

def unit_heads(values, attender_amount):
    shaped = values.astype(jnp.float32).reshape(values.shape[:-1] + (attender_amount, values.shape[-1] // attender_amount))
    scaled = shaped * lax.rsqrt(lax.optimization_barrier(jnp.sum(shaped * shaped, axis=-1, keepdims=True)) + 1e-06)
    return scaled.astype(jnp.bfloat16).reshape(values.shape)

def blockify(array):
    size_x, size_y, size_z, channels = array.shape
    shaped = array.reshape(size_x // BLOCK, BLOCK, size_y // BLOCK, BLOCK, size_z // BLOCK, BLOCK, channels)
    shaped = shaped.transpose(0, 2, 4, 1, 3, 5, 6)
    return shaped.reshape(size_x // BLOCK, size_y // BLOCK, size_z // BLOCK, BLOCK ** 3, channels)

def unblockify(blocks):
    count_x, count_y, count_z, inner, channels = blocks.shape
    shaped = blocks.reshape(count_x, count_y, count_z, BLOCK, BLOCK, BLOCK, channels)
    shaped = shaped.transpose(0, 3, 1, 4, 2, 5, 6)
    return shaped.reshape(count_x * BLOCK, count_y * BLOCK, count_z * BLOCK, channels)

def reference(slab_feature_entries, depthwise_filter_coefficients, rootmean_scaling_factors, asking_projection_factors, lookup_projection_factors, content_projection_factors, final_projection_factors, softness_per_attender, adjacent_block_codes, filled_list_lengths):
    channels = D
    attender_amount = ATTENDER_COUNT
    padded = jnp.pad(slab_feature_entries, ((1, 1), (1, 1), (1, 1), (0, 0)))
    hidden = conv_sum(padded, depthwise_filter_coefficients, NX, NY, TZ)
    normed = rms_norm(hidden, rootmean_scaling_factors)
    queries = unit_heads(project(normed, asking_projection_factors), attender_amount)
    key_units = unit_heads(project(normed, lookup_projection_factors), attender_amount)
    value_all = project(normed, content_projection_factors)
    query_blocks = blockify(queries)
    block_pad = ((1, 1), (1, 1), (1, 1), (0, 0), (0, 0))
    keys_padded = jnp.pad(blockify(key_units), block_pad)
    values_padded = jnp.pad(blockify(value_all), block_pad)
    slot_index = jnp.arange(SLOTS, dtype=jnp.int32)
    in_use = slot_index[None, None, None, :] < filled_list_lengths[..., None]
    index_x = jnp.arange(BX, dtype=jnp.int32)[:, None, None]
    index_y = jnp.arange(BY, dtype=jnp.int32)[None, :, None]
    index_z = jnp.arange(BZ, dtype=jnp.int32)[None, None, :]
    masks = []
    for code_index, (step_x, step_y, step_z) in enumerate(OFFSETS):
        named = jnp.any((adjacent_block_codes == code_index) & in_use, axis=-1)
        inside = (index_x + step_x >= 0) & (index_x + step_x < BX) & (index_y + step_y >= 0) & (index_y + step_y < BY) & (index_z + step_z >= 0) & (index_z + step_z < BZ)
        masks.append((named & inside).astype(jnp.float32))
    permitted_pairs = jnp.stack(masks, axis=-1)
    inner = BLOCK ** 3

    def one_row(row_index):
        asking_site_index = lax.dynamic_index_in_dim(query_blocks, row_index, 0, False)
        asking_site_index = asking_site_index.reshape(BY, BZ, inner, attender_amount, HD).astype(jnp.float32)
        mask_row = lax.dynamic_index_in_dim(permitted_pairs, row_index, 0, False)
        weighted = jnp.zeros((BY, BZ, inner, attender_amount, HD), jnp.float32)
        totals = jnp.zeros((BY, BZ, attender_amount, inner), jnp.float32)
        for code_index, (step_x, step_y, step_z) in enumerate(OFFSETS):
            lookup_site_index = lax.dynamic_index_in_dim(keys_padded, row_index + 1 + step_x, 0, False)
            lookup_site_index = lookup_site_index[1 + step_y:1 + step_y + BY, 1 + step_z:1 + step_z + BZ]
            lookup_site_index = lookup_site_index.reshape(BY, BZ, inner, attender_amount, HD).astype(jnp.float32)
            value_row = lax.dynamic_index_in_dim(values_padded, row_index + 1 + step_x, 0, False)
            value_row = value_row[1 + step_y:1 + step_y + BY, 1 + step_z:1 + step_z + BZ]
            value_row = value_row.reshape(BY, BZ, inner, attender_amount, HD).astype(jnp.float32)
            affinity_raw_values = jnp.einsum('mpfeb,mpceb->mpefc', asking_site_index, lookup_site_index) * softness_per_attender[:, None, None]
            weight_matrix = jnp.exp(affinity_raw_values) * mask_row[:, :, code_index][:, :, None, None, None]
            totals = totals + lax.optimization_barrier(jnp.sum(weight_matrix, axis=-1))
            rounded = lax.optimization_barrier(weight_matrix.astype(jnp.bfloat16)).astype(jnp.float32)
            weighted = weighted + jnp.einsum('yzhqk,yzkhd->yzqhd', rounded, value_row)
        result = weighted / jnp.transpose(totals, (0, 1, 3, 2))[..., None]
        return result.astype(jnp.bfloat16).reshape(BY, BZ, inner, channels)
    attended_blocks = lax.map(one_row, jnp.arange(BX, dtype=jnp.int32))
    attended = unblockify(attended_blocks)
    update = jnp.dot(attended.reshape(-1, channels), final_projection_factors, preferred_element_type=jnp.float32)
    mixed = hidden.astype(jnp.float32) + update.reshape(NX, NY, TZ, channels)
    return mixed.astype(jnp.bfloat16)
```

```python
import math

import jax
import jax.numpy as jnp
from jax import lax
from jax.experimental import pallas as pl
from jax.experimental.pallas import tpu as pltpu
from jax.sharding import PartitionSpec as P

BLOCK = 4
MESH = pl.DeviceIdType.MESH
F32 = jnp.float32
BF16 = jnp.bfloat16
X_ROWS = (slice(0, 1), slice(1, 7), slice(7, 8))


def kernel(
    count_gx,
    count_gy,
    x_hbm,
    taps_hbm,
    gain_hbm,
    wq_hbm,
    wk_hbm,
    wv_hbm,
    wf_hbm,
    soft_hbm,
    codes_hbm,
    lens_hbm,
    out_hbm,
    out_ref,
    x_ref,
    taps_ref,
    gain_ref,
    wq_ref,
    wk_ref,
    wv_ref,
    wf_ref,
    soft_ref,
    codes_ref,
    lens_ref,
    framed,
    summed,
    rim_x,
    rim_y,
    rim_c,
    hidden,
    normed,
    near_x,
    near_y,
    query,
    key,
    value,
    key_x,
    value_x,
    key_y,
    value_y,
    attended,
    acc,
    tot,
    send_sem,
    recv_sem,
    load_sem,
    store_sem,
):
    operands = (
        (x_hbm, x_ref),
        (taps_hbm, taps_ref),
        (gain_hbm, gain_ref),
        (wk_hbm, wk_ref),
        (wv_hbm, wv_ref),
        (wq_hbm, wq_ref),
        (soft_hbm, soft_ref),
        (codes_hbm, codes_ref),
        (lens_hbm, lens_ref),
        (wf_hbm, wf_ref),
    )
    loads = [
        pltpu.make_async_copy(src, dst, load_sem.at[i]) for i, (src, dst) in enumerate(operands)
    ]
    for load in loads:
        load.start()
    gx = lax.axis_index("gx")
    gy = lax.axis_index("gy")
    has_x = (gx > 0, gx < count_gx - 1)
    has_y = (gy > 0, gy < count_gy - 1)
    step = (-1, 1)

    def target(dx, dy):
        return {"gx": gx + dx, "gy": gy + dy}

    def exists(dx, dy):
        conds = []
        if dx:
            conds.append(has_x[(dx + 1) // 2])
        if dy:
            conds.append(has_y[(dy + 1) // 2])
        return conds[0] if len(conds) == 1 else conds[0] & conds[1]

    around = [(dx, dy) for dx in (-1, 0, 1) for dy in (-1, 0, 1) if dx or dy]

    barrier = pltpu.get_barrier_semaphore()
    for dx, dy in around:

        @pl.when(exists(dx, dy))
        def _():
            pl.semaphore_signal(barrier, inc=1, device_id=target(dx, dy), device_id_type=MESH)

    span_x = 1 + has_x[0].astype(jnp.int32) + has_x[1].astype(jnp.int32)
    span_y = 1 + has_y[0].astype(jnp.int32) + has_y[1].astype(jnp.int32)
    pl.semaphore_wait(barrier, span_x * span_y - 1)

    def copy(src, dst, out_slot, in_slot, dx, dy):
        return pltpu.make_async_remote_copy(
            src_ref=src,
            dst_ref=dst,
            send_sem=send_sem.at[out_slot],
            recv_sem=recv_sem.at[in_slot],
            device_id=target(dx, dy),
            device_id_type=MESH,
        )

    rims = []
    landing = {}
    for side in (0, 1):
        other = 1 - side
        rims.append((step[side], 0, x_hbm.at[7 * side], rim_x.at[other], side, other))
        landing[side] = (step[side], 0, rim_x.at[side])
    for side in (0, 1):
        for side_y in (0, 1):
            at = 2 * side + side_y
            rims.append(
                (
                    step[side],
                    step[side_y],
                    x_hbm.at[7 * side, 7 * side_y],
                    rim_c.at[3 - at],
                    4 + at,
                    4 + 3 - at,
                )
            )
            landing[4 + at] = (step[side], step[side_y], rim_c.at[at])
    for side in (0, 1):
        other = 1 - side
        rims.append((0, step[side], x_hbm.at[:, 7 * side], rim_y.at[other], 2 + side, 2 + other))
        landing[2 + side] = (0, step[side], rim_y.at[side])

    def face_y(side, at):
        other = 1 - side
        return (
            0,
            step[side],
            normed.at[4 * side + at],
            near_y.at[other, at],
            8 + 4 * side + at,
            8 + 4 * other + at,
        )

    def face_x(side, part):
        other = 1 - side
        rows = X_ROWS[part]
        return (
            step[side],
            0,
            normed.at[rows, side],
            near_x.at[other, rows],
            16 + 3 * side + part,
            16 + 3 * other + part,
        )

    for side in (0, 1):
        for at in range(4):
            landing[8 + 4 * side + at] = (0, step[side], near_y.at[side, at])
        for part in range(3):
            landing[16 + 3 * side + part] = (step[side], 0, near_x.at[side, X_ROWS[part]])

    def start(item):
        dx, dy, src, dst, out_slot, in_slot = item

        @pl.when(exists(dx, dy))
        def _():
            copy(src, dst, out_slot, in_slot, dx, dy).start()

    def finish_send(item):
        dx, dy, src, dst, out_slot, in_slot = item

        @pl.when(exists(dx, dy))
        def _():
            copy(src, dst, out_slot, in_slot, dx, dy).wait_send()

    def arrive(slots, landed, absent=None):
        dx, dy, _ = landing[slots[0]]

        @pl.when(exists(dx, dy))
        def _():
            for slot in slots:
                buffer = landing[slot][2]
                copy(buffer, buffer, slot, slot, dx, dy).wait_recv()
            landed()

        if absent is not None:

            @pl.when(jnp.logical_not(exists(dx, dy)))
            def _():
                absent()

    for item in rims:
        start(item)

    for load in loads[:3]:
        load.wait()

    for at in (0, 9):
        framed[at] = jnp.zeros((10, 8, 512), F32)
        framed[:, at] = jnp.zeros((10, 8, 512), F32)

    @pl.loop(0, 8)
    def _(x):
        framed[1:9, x + 1] = x_ref[x].astype(F32)

    def add_taps(pieces, lanes):
        sums = [None, None, None]
        for a, b, piece in pieces:
            for c in range(3):
                tap = 9 * a + 3 * b + c
                coefficient = taps_ref[tap : tap + 1, lanes]
                if piece.ndim == 3:
                    coefficient = coefficient.reshape(1, 1, 128)
                term = piece * coefficient
                sums[c] = term if sums[c] is None else sums[c] + term
        axis = sums[0].ndim - 2
        depth_at = lax.broadcasted_iota(jnp.int32, sums[0].shape, axis)
        low = jnp.where(depth_at > 0, pltpu.roll(sums[0], 1, axis), 0.0)
        high = jnp.where(depth_at < 7, pltpu.roll(sums[2], 7, axis), 0.0)
        return sums[1] + low + high

    groups = [slice(128 * group, 128 * group + 128) for group in range(4)]

    @pl.loop(0, 8)
    def _(y):
        for lanes in groups:
            pieces = [
                (a, b, framed[y + b, a : a + 8, :, lanes]) for a in range(3) for b in range(3)
            ]
            own = framed[y + 1, 1:9, :, lanes]
            summed[y, :, :, lanes] = own + add_taps(pieces, lanes)

    for side in (0, 1):

        def landed(side=side):
            framed[1:9, 9 * side] = rim_x[side].astype(F32)
            for lanes in groups:
                pieces = [
                    (2 * side, b, framed[b : b + 8, 9 * side, :, lanes]) for b in range(3)
                ]
                before = summed[:, 7 * side, :, lanes]
                summed[:, 7 * side, :, lanes] = before + add_taps(pieces, lanes)

        arrive((side,), landed)

    half_at = lax.broadcasted_iota(jnp.int32, (4, 8, 512), 1) < 4
    gain = gain_ref[...].reshape(1, 1, 512)

    def finish_row(y):
        rows = summed[y].astype(BF16).astype(F32)
        pairs = rows.reshape(4, 2, 8, 512)
        even, odd = pairs[:, 0], pairs[:, 1]
        lower = jnp.where(half_at, even, pltpu.roll(odd, 4, 1))
        upper = jnp.where(half_at, pltpu.roll(even, 4, 1), odd)
        for bz, part in ((0, lower), (1, upper)):
            scale = lax.rsqrt(jnp.mean(part * part, axis=-1, keepdims=True) + 1e-05)
            unit = (part * scale * gain).reshape(2, 16, 512).astype(BF16)
            part = part.reshape(2, 16, 512).astype(BF16)
            for bx in (0, 1):
                hidden[y, bx, bz] = part[bx]
                normed[y, bx, bz] = unit[bx]

    @pl.loop(0, 3)
    def _(i):
        finish_row(1 + i)
        start(face_y(0, 1 + i))
        finish_row(6 - i)
        start(face_y(1, 2 - i))

    for side in (0, 1):
        start(face_x(side, 1))

    for load in loads[3:6]:
        load.wait()
    row = lax.broadcasted_iota(jnp.int32, (256, 256), 0) // 64
    column = lax.broadcasted_iota(jnp.int32, (256, 256), 1) // 64
    same_head = (row == column).astype(F32).astype(BF16)
    head_at = lax.broadcasted_iota(jnp.int32, (64, 256), 1) // 64
    head_of = lax.broadcasted_iota(jnp.int32, (16, 256), 1) // 64

    def units(raw):
        squares = (raw * raw).astype(BF16)
        sums = jnp.dot(squares, same_head, preferred_element_type=F32)
        return raw * lax.rsqrt(sums + 1e-06)

    def project(tokens, w_ref, quad):
        lanes = slice(256 * quad, 256 * quad + 256)
        return jnp.dot(tokens, w_ref[:, lanes], preferred_element_type=F32)

    def gather(parts):
        return jnp.concatenate([part[...].reshape(-1, 512) for part in parts], axis=0)

    def scatter(parts, lanes, values):
        at = 0
        for part in parts:
            shape = part.shape[:-1] + (256,)
            extent = math.prod(part.shape[:-1])
            part[..., lanes] = values[at : at + extent].reshape(shape)
            at += extent

    def keys_values(src, key_dst, value_dst):
        tokens = gather(src)
        for quad in (0, 1):
            lanes = slice(256 * quad, 256 * quad + 256)
            scatter(key_dst, lanes, units(project(tokens, wk_ref, quad)).astype(BF16))
            scatter(value_dst, lanes, project(tokens, wv_ref, quad).astype(BF16))

    def own_rows(spans):
        src = [normed.at[span] for span in spans]
        rows = [y for span in spans for y in range(span.start, span.stop)]
        tokens = gather(src)
        for quad in (0, 1):
            unit = units(project(tokens, wq_ref, quad)).reshape(len(rows), 2, 2, 16, 256)
            for i, y in enumerate(rows):
                by, yi = y // 4, y % 4
                for bx in (0, 1):
                    for bz in (0, 1):
                        for j in range(4):
                            kept = jnp.where(head_of == j, unit[i, bx, bz], 0.0)
                            at = 64 * j + 16 * yi
                            query[bx, by, bz, quad, at : at + 16] = kept.astype(BF16)
        keys_values(src, [key.at[s] for s in spans], [value.at[s] for s in spans])

    own_rows([slice(1, 4), slice(4, 7)])

    def fill(index, ref):
        def landed():
            framed[index] = ref[...].astype(F32)

        return landed

    for side_y in (0, 1):
        at = 9 * side_y
        for side in (0, 1):
            slot = 2 * side + side_y
            arrive((4 + slot,), fill((at, 9 * side), rim_c.at[slot]))
        arrive((2 + side_y,), fill((at, slice(1, 9)), rim_y.at[side_y]))
        y = 7 * side_y
        for lanes in groups:
            pieces = [(a, 2 * side_y, framed[at, a : a + 8, :, lanes]) for a in range(3)]
            summed[y, :, :, lanes] = summed[y, :, :, lanes] + add_taps(pieces, lanes)
        finish_row(y)
        start(face_y(side_y, 3 * side_y))
        for side in (0, 1):
            start(face_x(side, 2 * side_y))

    own_rows([slice(0, 1), slice(7, 8)])

    for load in loads[6:]:
        load.wait()
    log2e = math.log2(math.e)
    slots = codes_ref.shape[3]

    def attend(bx, by, bz, near):
        extent = 64 * len(near)
        slot_at = lax.broadcasted_iota(jnp.int32, (1, extent), 1) // 64
        named = jnp.full((1, extent), -2, jnp.int32)
        for j, (code, _, _) in enumerate(near):
            named = jnp.where(slot_at == j, code, named)
        mask = jnp.zeros((1, extent), F32)
        length = lens_ref[bx, by, bz]
        for s in range(slots):
            code = jnp.where(s < length, codes_ref[bx, by, bz, s], -1)
            mask = jnp.where(named == code, 1.0, mask)
        outs, sums = [], []
        for quad in (0, 1):
            lanes = slice(256 * quad, 256 * quad + 256)
            keys = jnp.concatenate([k[..., lanes].reshape(64, 256) for _, k, _ in near], axis=0)
            values = jnp.concatenate([v[..., lanes].reshape(64, 256) for _, _, v in near], axis=0)
            score = lax.dot_general(
                query[bx, by, bz, quad],
                keys,
                (((1,), (1,)), ((), ())),
                preferred_element_type=F32,
            )
            weights, totals = [], []
            for j in range(4):
                factor = soft_ref[4 * quad + j] * log2e
                weight = jnp.exp2(score[64 * j : 64 * j + 64] * factor) * mask
                totals.append(jnp.sum(weight, axis=-1, keepdims=True))
                weights.append(weight.astype(BF16))
            mixed = jnp.dot(
                jnp.concatenate(weights, axis=0), values, preferred_element_type=F32
            )
            out = mixed[0:64]
            total = jnp.broadcast_to(totals[0], (64, 256))
            for j in range(1, 4):
                out = jnp.where(head_at == j, mixed[64 * j : 64 * j + 64], out)
                total = jnp.where(head_at == j, totals[j], total)
            outs.append(out)
            sums.append(total)
        return outs, sums

    def attend_own(bx, by, bz):
        own, beside = pl.ds(4 * by, 4), pl.ds(4 - 4 * by, 4)
        near = [
            (6 * bz, key.at[own, bx, 0], value.at[own, bx, 0]),
            (5 * (1 - bz), key.at[own, bx, 1], value.at[own, bx, 1]),
            (1 + bx, key.at[own, 1 - bx, bz], value.at[own, 1 - bx, bz]),
            (3 + by, key.at[beside, bx, bz], value.at[beside, bx, bz]),
        ]
        outs, sums = attend(bx, by, bz, near)
        for quad in (0, 1):
            lanes = slice(256 * quad, 256 * quad + 256)
            acc[bx, by, bz, :, lanes] = outs[quad]
            tot[bx, by, bz, :, lanes] = sums[quad]

    for by in (0, 1):
        for bx in (0, 1):
            for bz in (0, 1):
                attend_own(bx, by, bz)

    def clear(*refs):
        def absent():
            for ref in refs:
                ref[...] = jnp.zeros(ref.shape, BF16)

        return absent

    for side in (0, 1):
        arrive(
            tuple(16 + 3 * side + part for part in range(3)),
            lambda side=side: keys_values(
                [near_x.at[side]], [key_x.at[side]], [value_x.at[side]]
            ),
            clear(key_x.at[side], value_x.at[side]),
        )
    for side in (0, 1):
        early = (0, 1, 2) if side == 0 else (1, 2, 3)
        span = slice(early[0], early[-1] + 1)
        arrive(
            tuple(8 + 4 * side + at for at in early),
            lambda side=side, span=span: keys_values(
                [near_y.at[side, span]], [key_y.at[side, span]], [value_y.at[side, span]]
            ),
            clear(key_y.at[side, span], value_y.at[side, span]),
        )
    for side in (0, 1):
        at = 3 - 3 * side
        arrive(
            (8 + 4 * side + at,),
            lambda side=side, at=at: keys_values(
                [near_y.at[side, at]], [key_y.at[side, at]], [value_y.at[side, at]]
            ),
            clear(key_y.at[side, at], value_y.at[side, at]),
        )

    in_x = [has.astype(jnp.int32) for has in has_x]
    in_y = [has.astype(jnp.int32) for has in has_y]

    def attend_near(bx, by, bz):
        rows = pl.ds(4 * by, 4)
        near = [
            (
                jnp.where(in_x[bx] > 0, 2 - bx, -2),
                key_x.at[bx, rows, bz],
                value_x.at[bx, rows, bz],
            ),
            (
                jnp.where(in_y[by] > 0, 4 - by, -2),
                key_y.at[by, :, bx, bz],
                value_y.at[by, :, bx, bz],
            ),
        ]
        outs, sums = attend(bx, by, bz, near)
        for quad in (0, 1):
            lanes = slice(256 * quad, 256 * quad + 256)
            result = (acc[bx, by, bz, :, lanes] + outs[quad]) / (
                tot[bx, by, bz, :, lanes] + sums[quad]
            )
            attended[rows, bx, bz, :, lanes] = result.reshape(4, 16, 256).astype(BF16)

    stores = []
    for by in (0, 1):
        for bx in (0, 1):
            for bz in (0, 1):
                attend_near(bx, by, bz)
        rows = pl.ds(4 * by, 4)
        update = jnp.dot(
            attended[rows].reshape(256, 512), wf_ref[...], preferred_element_type=F32
        )
        mixed = hidden[rows].reshape(256, 512).astype(F32) + update
        mixed = mixed.reshape(4, 2, 2, 2, 8, 512)
        lower = mixed[:, :, 0].reshape(16, 8, 512)
        upper = mixed[:, :, 1].reshape(16, 8, 512)
        split = lax.broadcasted_iota(jnp.int32, (16, 8, 512), 1) < 4
        even = jnp.where(split, lower, pltpu.roll(upper, 4, 1)).astype(BF16)
        odd = jnp.where(split, pltpu.roll(lower, 4, 1), upper).astype(BF16)
        for yi in range(4):
            for pair in range(4):
                out_ref[2 * pair, 4 * by + yi] = even[4 * yi + pair]
                out_ref[2 * pair + 1, 4 * by + yi] = odd[4 * yi + pair]
        store = pltpu.make_async_copy(out_ref.at[:, rows], out_hbm.at[:, rows], store_sem.at[by])
        store.start()
        stores.append(store)

    for item in rims:
        finish_send(item)
    for side in (0, 1):
        for at in range(4):
            finish_send(face_y(side, at))
        for part in range(3):
            finish_send(face_x(side, part))
    for store in stores:
        store.wait()


def solution(mesh):
    count_gx = mesh.shape["gx"]
    count_gy = mesh.shape["gy"]

    def body(x, taps, gain, wq, wk, wv, wf, soft, codes, lens):
        hbm = pl.BlockSpec(memory_space=pltpu.HBM)

        def run(*refs):
            kernel(count_gx, count_gy, *refs)

        return pl.pallas_call(
            run,
            out_shape=jax.ShapeDtypeStruct(x.shape, BF16),
            in_specs=[hbm] * 10,
            out_specs=hbm,
            scratch_shapes=[pltpu.VMEM(a.shape, a.dtype) for a in (x, x, taps, gain, wq, wk, wv, wf)]
            + [pltpu.SMEM(a.shape, a.dtype) for a in (soft, codes, lens)]
            + [
                pltpu.VMEM((10, 10, 8, 512), F32),
                pltpu.VMEM((8, 8, 8, 512), F32),
                pltpu.VMEM((2, 8, 8, 512), BF16),
                pltpu.VMEM((2, 8, 8, 512), BF16),
                pltpu.VMEM((4, 8, 512), BF16),
                pltpu.VMEM((8, 2, 2, 16, 512), BF16),
                pltpu.VMEM((8, 2, 2, 16, 512), BF16),
                pltpu.VMEM((2, 8, 2, 16, 512), BF16),
                pltpu.VMEM((2, 4, 2, 2, 16, 512), BF16),
                pltpu.VMEM((2, 2, 2, 2, 256, 256), BF16),
                pltpu.VMEM((8, 2, 2, 16, 512), BF16),
                pltpu.VMEM((8, 2, 2, 16, 512), BF16),
                pltpu.VMEM((2, 8, 2, 16, 512), BF16),
                pltpu.VMEM((2, 8, 2, 16, 512), BF16),
                pltpu.VMEM((2, 4, 2, 2, 16, 512), BF16),
                pltpu.VMEM((2, 4, 2, 2, 16, 512), BF16),
                pltpu.VMEM((8, 2, 2, 16, 512), BF16),
            ]
            + [pltpu.VMEM((2, 2, 2, 64, 512), F32)] * 2
            + [pltpu.SemaphoreType.DMA((count,)) for count in (22, 22, 10, 2)],
            compiler_params=pltpu.CompilerParams(
                collective_id=0, has_side_effects=True, vmem_limit_bytes=60 * 1024 * 1024
            ),
            cost_estimate=pl.CostEstimate(
                flops=4 * 10**9, bytes_accessed=4 * 10**6, transcendentals=2 * 10**6
            ),
        )(x, taps, gain, wq, wk, wv, wf, soft, codes, lens)

    in_specs = (
        P(("slab", "gx"), "gy", None, None),
        P(),
        P(),
        P(),
        P(),
        P(),
        P(),
        P(),
        P(("slab", "gx"), "gy", None, None),
        P(("slab", "gx"), "gy", None),
    )
    out_specs = P(("slab", "gx"), "gy", None, None)
    return jax.shard_map(body, mesh=mesh, in_specs=in_specs, out_specs=out_specs, check_vma=False)
```

```python
import math

import jax
import jax.numpy as jnp
from jax import lax
from jax.experimental import pallas as pl
from jax.experimental.pallas import tpu as pltpu
from jax.sharding import PartitionSpec as P

BLOCK = 4
MESH = pl.DeviceIdType.MESH
F32 = jnp.float32
BF16 = jnp.bfloat16
X_ROWS = (slice(0, 1), slice(1, 7), slice(7, 8))


def kernel(
    count_gx,
    count_gy,
    x_hbm,
    taps_hbm,
    gain_hbm,
    wq_hbm,
    wk_hbm,
    wv_hbm,
    soft_hbm,
    codes_hbm,
    lens_hbm,
    hidden,
    attended,
    x_ref,
    taps_ref,
    gain_ref,
    wq_ref,
    wk_ref,
    wv_ref,
    soft_ref,
    codes_ref,
    lens_ref,
    framed,
    summed,
    rim_x,
    rim_y,
    rim_c,
    normed,
    near_x,
    near_y,
    query,
    key,
    value,
    key_x,
    value_x,
    key_y,
    value_y,
    acc,
    tot,
    send_sem,
    recv_sem,
    load_sem,
):
    operands = (
        (x_hbm, x_ref),
        (taps_hbm, taps_ref),
        (gain_hbm, gain_ref),
        (wk_hbm, wk_ref),
        (wv_hbm, wv_ref),
        (wq_hbm, wq_ref),
        (soft_hbm, soft_ref),
        (codes_hbm, codes_ref),
        (lens_hbm, lens_ref),
    )
    loads = [
        pltpu.make_async_copy(src, dst, load_sem.at[i]) for i, (src, dst) in enumerate(operands)
    ]
    for load in loads:
        load.start()
    gx = lax.axis_index("gx")
    gy = lax.axis_index("gy")
    has_x = (gx > 0, gx < count_gx - 1)
    has_y = (gy > 0, gy < count_gy - 1)
    step = (-1, 1)

    def target(dx, dy):
        return {"gx": gx + dx, "gy": gy + dy}

    def exists(dx, dy):
        conds = []
        if dx:
            conds.append(has_x[(dx + 1) // 2])
        if dy:
            conds.append(has_y[(dy + 1) // 2])
        return conds[0] if len(conds) == 1 else conds[0] & conds[1]

    around = [(dx, dy) for dx in (-1, 0, 1) for dy in (-1, 0, 1) if dx or dy]

    barrier = pltpu.get_barrier_semaphore()
    for dx, dy in around:

        @pl.when(exists(dx, dy))
        def _():
            pl.semaphore_signal(barrier, inc=1, device_id=target(dx, dy), device_id_type=MESH)

    span_x = 1 + has_x[0].astype(jnp.int32) + has_x[1].astype(jnp.int32)
    span_y = 1 + has_y[0].astype(jnp.int32) + has_y[1].astype(jnp.int32)
    pl.semaphore_wait(barrier, span_x * span_y - 1)

    def copy(src, dst, out_slot, in_slot, dx, dy):
        return pltpu.make_async_remote_copy(
            src_ref=src,
            dst_ref=dst,
            send_sem=send_sem.at[out_slot],
            recv_sem=recv_sem.at[in_slot],
            device_id=target(dx, dy),
            device_id_type=MESH,
        )

    rims = []
    landing = {}
    for side in (0, 1):
        other = 1 - side
        rims.append((step[side], 0, x_hbm.at[7 * side], rim_x.at[other], side, other))
        landing[side] = (step[side], 0, rim_x.at[side])
    for side in (0, 1):
        for side_y in (0, 1):
            at = 2 * side + side_y
            rims.append(
                (
                    step[side],
                    step[side_y],
                    x_hbm.at[7 * side, 7 * side_y],
                    rim_c.at[3 - at],
                    4 + at,
                    4 + 3 - at,
                )
            )
            landing[4 + at] = (step[side], step[side_y], rim_c.at[at])
    for side in (0, 1):
        other = 1 - side
        rims.append((0, step[side], x_hbm.at[:, 7 * side], rim_y.at[other], 2 + side, 2 + other))
        landing[2 + side] = (0, step[side], rim_y.at[side])

    def face_y(side, at):
        other = 1 - side
        return (
            0,
            step[side],
            normed.at[4 * side + at],
            near_y.at[other, at],
            8 + 4 * side + at,
            8 + 4 * other + at,
        )

    def face_x(side, part):
        other = 1 - side
        rows = X_ROWS[part]
        return (
            step[side],
            0,
            normed.at[rows, side],
            near_x.at[other, rows],
            16 + 3 * side + part,
            16 + 3 * other + part,
        )

    for side in (0, 1):
        for at in range(4):
            landing[8 + 4 * side + at] = (0, step[side], near_y.at[side, at])
        for part in range(3):
            landing[16 + 3 * side + part] = (step[side], 0, near_x.at[side, X_ROWS[part]])

    def start(item):
        dx, dy, src, dst, out_slot, in_slot = item

        @pl.when(exists(dx, dy))
        def _():
            copy(src, dst, out_slot, in_slot, dx, dy).start()

    def finish_send(item):
        dx, dy, src, dst, out_slot, in_slot = item

        @pl.when(exists(dx, dy))
        def _():
            copy(src, dst, out_slot, in_slot, dx, dy).wait_send()

    def arrive(slots, landed, absent=None):
        dx, dy, _ = landing[slots[0]]

        @pl.when(exists(dx, dy))
        def _():
            for slot in slots:
                buffer = landing[slot][2]
                copy(buffer, buffer, slot, slot, dx, dy).wait_recv()
            landed()

        if absent is not None:

            @pl.when(jnp.logical_not(exists(dx, dy)))
            def _():
                absent()

    for item in rims:
        start(item)

    for load in loads[:3]:
        load.wait()

    for at in (0, 9):
        framed[at] = jnp.zeros((10, 8, 512), F32)
        framed[:, at] = jnp.zeros((10, 8, 512), F32)

    @pl.loop(0, 8)
    def _(x):
        framed[1:9, x + 1] = x_ref[x].astype(F32)

    def add_taps(pieces, lanes):
        sums = [None, None, None]
        for a, b, piece in pieces:
            for c in range(3):
                tap = 9 * a + 3 * b + c
                coefficient = taps_ref[tap : tap + 1, lanes]
                if piece.ndim == 3:
                    coefficient = coefficient.reshape(1, 1, 128)
                term = piece * coefficient
                sums[c] = term if sums[c] is None else sums[c] + term
        axis = sums[0].ndim - 2
        depth_at = lax.broadcasted_iota(jnp.int32, sums[0].shape, axis)
        low = jnp.where(depth_at > 0, pltpu.roll(sums[0], 1, axis), 0.0)
        high = jnp.where(depth_at < 7, pltpu.roll(sums[2], 7, axis), 0.0)
        return sums[1] + low + high

    groups = [slice(128 * group, 128 * group + 128) for group in range(4)]

    @pl.loop(0, 8)
    def _(y):
        for lanes in groups:
            pieces = [
                (a, b, framed[y + b, a : a + 8, :, lanes]) for a in range(3) for b in range(3)
            ]
            own = framed[y + 1, 1:9, :, lanes]
            summed[y, :, :, lanes] = own + add_taps(pieces, lanes)

    for side in (0, 1):

        def landed(side=side):
            framed[1:9, 9 * side] = rim_x[side].astype(F32)
            for lanes in groups:
                pieces = [
                    (2 * side, b, framed[b : b + 8, 9 * side, :, lanes]) for b in range(3)
                ]
                before = summed[:, 7 * side, :, lanes]
                summed[:, 7 * side, :, lanes] = before + add_taps(pieces, lanes)

        arrive((side,), landed)

    half_at = lax.broadcasted_iota(jnp.int32, (4, 8, 512), 1) < 4
    gain = gain_ref[...].reshape(1, 1, 512)

    def finish_row(y):
        rows = summed[y].astype(BF16).astype(F32)
        pairs = rows.reshape(4, 2, 8, 512)
        even, odd = pairs[:, 0], pairs[:, 1]
        lower = jnp.where(half_at, even, pltpu.roll(odd, 4, 1))
        upper = jnp.where(half_at, pltpu.roll(even, 4, 1), odd)
        for bz, part in ((0, lower), (1, upper)):
            scale = lax.rsqrt(jnp.mean(part * part, axis=-1, keepdims=True) + 1e-05)
            unit = (part * scale * gain).reshape(2, 16, 512).astype(BF16)
            part = part.reshape(2, 16, 512).astype(BF16)
            for bx in (0, 1):
                hidden[y, bx, bz] = part[bx]
                normed[y, bx, bz] = unit[bx]

    @pl.loop(0, 3)
    def _(i):
        finish_row(1 + i)
        start(face_y(0, 1 + i))
        finish_row(6 - i)
        start(face_y(1, 2 - i))

    for side in (0, 1):
        start(face_x(side, 1))

    for load in loads[3:6]:
        load.wait()
    row = lax.broadcasted_iota(jnp.int32, (256, 256), 0) // 64
    column = lax.broadcasted_iota(jnp.int32, (256, 256), 1) // 64
    same_head = (row == column).astype(F32).astype(BF16)
    head_at = lax.broadcasted_iota(jnp.int32, (64, 256), 1) // 64
    head_of = lax.broadcasted_iota(jnp.int32, (16, 256), 1) // 64

    def units(raw):
        squares = (raw * raw).astype(BF16)
        sums = jnp.dot(squares, same_head, preferred_element_type=F32)
        return raw * lax.rsqrt(sums + 1e-06)

    def project(tokens, w_ref, quad):
        lanes = slice(256 * quad, 256 * quad + 256)
        return jnp.dot(tokens, w_ref[:, lanes], preferred_element_type=F32)

    def gather(parts):
        return jnp.concatenate([part[...].reshape(-1, 512) for part in parts], axis=0)

    def scatter(parts, lanes, values):
        at = 0
        for part in parts:
            shape = part.shape[:-1] + (256,)
            extent = math.prod(part.shape[:-1])
            part[..., lanes] = values[at : at + extent].reshape(shape)
            at += extent

    def keys_values(src, key_dst, value_dst):
        tokens = gather(src)
        for quad in (0, 1):
            lanes = slice(256 * quad, 256 * quad + 256)
            scatter(key_dst, lanes, units(project(tokens, wk_ref, quad)).astype(BF16))
            scatter(value_dst, lanes, project(tokens, wv_ref, quad).astype(BF16))

    def own_rows(spans):
        src = [normed.at[span] for span in spans]
        rows = [y for span in spans for y in range(span.start, span.stop)]
        tokens = gather(src)
        for quad in (0, 1):
            unit = units(project(tokens, wq_ref, quad)).reshape(len(rows), 2, 2, 16, 256)
            for i, y in enumerate(rows):
                by, yi = y // 4, y % 4
                for bx in (0, 1):
                    for bz in (0, 1):
                        for j in range(4):
                            kept = jnp.where(head_of == j, unit[i, bx, bz], 0.0)
                            at = 64 * j + 16 * yi
                            query[bx, by, bz, quad, at : at + 16] = kept.astype(BF16)
        keys_values(src, [key.at[s] for s in spans], [value.at[s] for s in spans])

    own_rows([slice(1, 4), slice(4, 7)])

    def fill(index, ref):
        def landed():
            framed[index] = ref[...].astype(F32)

        return landed

    for side_y in (0, 1):
        at = 9 * side_y
        for side in (0, 1):
            slot = 2 * side + side_y
            arrive((4 + slot,), fill((at, 9 * side), rim_c.at[slot]))
        arrive((2 + side_y,), fill((at, slice(1, 9)), rim_y.at[side_y]))
        y = 7 * side_y
        for lanes in groups:
            pieces = [(a, 2 * side_y, framed[at, a : a + 8, :, lanes]) for a in range(3)]
            summed[y, :, :, lanes] = summed[y, :, :, lanes] + add_taps(pieces, lanes)
        finish_row(y)
        start(face_y(side_y, 3 * side_y))
        for side in (0, 1):
            start(face_x(side, 2 * side_y))

    own_rows([slice(0, 1), slice(7, 8)])

    for load in loads[6:]:
        load.wait()
    log2e = math.log2(math.e)
    slots = codes_ref.shape[3]

    def attend(bx, by, bz, near):
        extent = 64 * len(near)
        slot_at = lax.broadcasted_iota(jnp.int32, (1, extent), 1) // 64
        named = jnp.full((1, extent), -2, jnp.int32)
        for j, (code, _, _) in enumerate(near):
            named = jnp.where(slot_at == j, code, named)
        mask = jnp.zeros((1, extent), F32)
        length = lens_ref[bx, by, bz]
        for s in range(slots):
            code = jnp.where(s < length, codes_ref[bx, by, bz, s], -1)
            mask = jnp.where(named == code, 1.0, mask)
        outs, sums = [], []
        for quad in (0, 1):
            lanes = slice(256 * quad, 256 * quad + 256)
            keys = jnp.concatenate([k[..., lanes].reshape(64, 256) for _, k, _ in near], axis=0)
            values = jnp.concatenate([v[..., lanes].reshape(64, 256) for _, _, v in near], axis=0)
            score = lax.dot_general(
                query[bx, by, bz, quad],
                keys,
                (((1,), (1,)), ((), ())),
                preferred_element_type=F32,
            )
            weights, totals = [], []
            for j in range(4):
                factor = soft_ref[4 * quad + j] * log2e
                weight = jnp.exp2(score[64 * j : 64 * j + 64] * factor) * mask
                totals.append(jnp.sum(weight, axis=-1, keepdims=True))
                weights.append(weight.astype(BF16))
            mixed = jnp.dot(
                jnp.concatenate(weights, axis=0), values, preferred_element_type=F32
            )
            out = mixed[0:64]
            total = jnp.broadcast_to(totals[0], (64, 256))
            for j in range(1, 4):
                out = jnp.where(head_at == j, mixed[64 * j : 64 * j + 64], out)
                total = jnp.where(head_at == j, totals[j], total)
            outs.append(out)
            sums.append(total)
        return outs, sums

    def attend_own(bx, by, bz):
        own, beside = pl.ds(4 * by, 4), pl.ds(4 - 4 * by, 4)
        near = [
            (6 * bz, key.at[own, bx, 0], value.at[own, bx, 0]),
            (5 * (1 - bz), key.at[own, bx, 1], value.at[own, bx, 1]),
            (1 + bx, key.at[own, 1 - bx, bz], value.at[own, 1 - bx, bz]),
            (3 + by, key.at[beside, bx, bz], value.at[beside, bx, bz]),
        ]
        outs, sums = attend(bx, by, bz, near)
        for quad in (0, 1):
            lanes = slice(256 * quad, 256 * quad + 256)
            acc[bx, by, bz, :, lanes] = outs[quad]
            tot[bx, by, bz, :, lanes] = sums[quad]

    for by in (0, 1):
        for bx in (0, 1):
            for bz in (0, 1):
                attend_own(bx, by, bz)

    def clear(*refs):
        def absent():
            for ref in refs:
                ref[...] = jnp.zeros(ref.shape, BF16)

        return absent

    for side in (0, 1):
        arrive(
            tuple(16 + 3 * side + part for part in range(3)),
            lambda side=side: keys_values(
                [near_x.at[side]], [key_x.at[side]], [value_x.at[side]]
            ),
            clear(key_x.at[side], value_x.at[side]),
        )
    for side in (0, 1):
        early = (0, 1, 2) if side == 0 else (1, 2, 3)
        span = slice(early[0], early[-1] + 1)
        arrive(
            tuple(8 + 4 * side + at for at in early),
            lambda side=side, span=span: keys_values(
                [near_y.at[side, span]], [key_y.at[side, span]], [value_y.at[side, span]]
            ),
            clear(key_y.at[side, span], value_y.at[side, span]),
        )
    for side in (0, 1):
        at = 3 - 3 * side
        arrive(
            (8 + 4 * side + at,),
            lambda side=side, at=at: keys_values(
                [near_y.at[side, at]], [key_y.at[side, at]], [value_y.at[side, at]]
            ),
            clear(key_y.at[side, at], value_y.at[side, at]),
        )

    in_x = [has.astype(jnp.int32) for has in has_x]
    in_y = [has.astype(jnp.int32) for has in has_y]

    def attend_near(bx, by, bz):
        rows = pl.ds(4 * by, 4)
        near = [
            (
                jnp.where(in_x[bx] > 0, 2 - bx, -2),
                key_x.at[bx, rows, bz],
                value_x.at[bx, rows, bz],
            ),
            (
                jnp.where(in_y[by] > 0, 4 - by, -2),
                key_y.at[by, :, bx, bz],
                value_y.at[by, :, bx, bz],
            ),
        ]
        outs, sums = attend(bx, by, bz, near)
        for quad in (0, 1):
            lanes = slice(256 * quad, 256 * quad + 256)
            result = (acc[bx, by, bz, :, lanes] + outs[quad]) / (
                tot[bx, by, bz, :, lanes] + sums[quad]
            )
            attended[rows, bx, bz, :, lanes] = result.reshape(4, 16, 256).astype(BF16)

    for by in (0, 1):
        for bx in (0, 1):
            for bz in (0, 1):
                attend_near(bx, by, bz)
        rows = pl.ds(4 * by, 4)

    for item in rims:
        finish_send(item)
    for side in (0, 1):
        for at in range(4):
            finish_send(face_y(side, at))
        for part in range(3):
            finish_send(face_x(side, part))


def finish(hidden, attended, wf_ref, out_hbm, out_ref, store_sem):
    stores = []
    for by in (0, 1):
        rows = pl.ds(4 * by, 4)
        update = jnp.dot(
            attended[rows].reshape(256, 512), wf_ref[...], preferred_element_type=F32
        )
        mixed = hidden[rows].reshape(256, 512).astype(F32) + update
        mixed = mixed.reshape(4, 2, 2, 2, 8, 512)
        lower = mixed[:, :, 0].reshape(16, 8, 512)
        upper = mixed[:, :, 1].reshape(16, 8, 512)
        split = lax.broadcasted_iota(jnp.int32, (16, 8, 512), 1) < 4
        even = jnp.where(split, lower, pltpu.roll(upper, 4, 1)).astype(BF16)
        odd = jnp.where(split, pltpu.roll(lower, 4, 1), upper).astype(BF16)
        for yi in range(4):
            for pair in range(4):
                out_ref[2 * pair, 4 * by + yi] = even[4 * yi + pair]
                out_ref[2 * pair + 1, 4 * by + yi] = odd[4 * yi + pair]
        store = pltpu.make_async_copy(out_ref.at[:, rows], out_hbm.at[:, rows], store_sem.at[by])
        store.start()
        stores.append(store)
    for store in stores:
        store.wait()


def solution(mesh):
    count_gx = mesh.shape["gx"]
    count_gy = mesh.shape["gy"]

    def body(x, taps, gain, wq, wk, wv, wf, soft, codes, lens):
        hbm = pl.BlockSpec(memory_space=pltpu.HBM)

        def run(*refs):
            kernel(count_gx, count_gy, *refs)

        x, taps, gain, wq, wk, wv, soft, codes, lens = (
            pltpu.with_memory_space_constraint(a, pltpu.HBM)
            for a in (x, taps, gain, wq, wk, wv, soft, codes, lens)
        )
        hidden, attended = pl.pallas_call(
            run,
            out_shape=[pltpu.VMEM((8, 2, 2, 16, 512), BF16)] * 2,
            in_specs=[hbm] * 9,
            out_specs=[pl.BlockSpec(memory_space=pltpu.VMEM)] * 2,
            scratch_shapes=[pltpu.VMEM(a.shape, a.dtype) for a in (x, taps, gain, wq, wk, wv)]
            + [pltpu.SMEM(a.shape, a.dtype) for a in (soft, codes, lens)]
            + [
                pltpu.VMEM((10, 10, 8, 512), F32),
                pltpu.VMEM((8, 8, 8, 512), F32),
                pltpu.VMEM((2, 8, 8, 512), BF16),
                pltpu.VMEM((2, 8, 8, 512), BF16),
                pltpu.VMEM((4, 8, 512), BF16),
                pltpu.VMEM((8, 2, 2, 16, 512), BF16),
                pltpu.VMEM((2, 8, 2, 16, 512), BF16),
                pltpu.VMEM((2, 4, 2, 2, 16, 512), BF16),
                pltpu.VMEM((2, 2, 2, 2, 256, 256), BF16),
                pltpu.VMEM((8, 2, 2, 16, 512), BF16),
                pltpu.VMEM((8, 2, 2, 16, 512), BF16),
                pltpu.VMEM((2, 8, 2, 16, 512), BF16),
                pltpu.VMEM((2, 8, 2, 16, 512), BF16),
                pltpu.VMEM((2, 4, 2, 2, 16, 512), BF16),
                pltpu.VMEM((2, 4, 2, 2, 16, 512), BF16),
            ]
            + [pltpu.VMEM((2, 2, 2, 64, 512), F32)] * 2
            + [pltpu.SemaphoreType.DMA((count,)) for count in (22, 22, 9)],
            compiler_params=pltpu.CompilerParams(
                collective_id=0, has_side_effects=True, vmem_limit_bytes=32 * 1024 * 1024
            ),
            cost_estimate=pl.CostEstimate(
                flops=4 * 10**9, bytes_accessed=4 * 10**6, transcendentals=2 * 10**6
            ),
        )(x, taps, gain, wq, wk, wv, soft, codes, lens)
        vmem = pl.BlockSpec(memory_space=pltpu.VMEM)
        return pl.pallas_call(
            finish,
            out_shape=jax.ShapeDtypeStruct(x.shape, BF16),
            in_specs=[vmem, vmem, vmem],
            out_specs=hbm,
            scratch_shapes=[pltpu.VMEM(x.shape, BF16), pltpu.SemaphoreType.DMA((2,))],
            compiler_params=pltpu.CompilerParams(vmem_limit_bytes=8 * 1024 * 1024),
        )(hidden, attended, wf)

    in_specs = (
        P(("slab", "gx"), "gy", None, None),
        P(),
        P(),
        P(),
        P(),
        P(),
        P(),
        P(),
        P(("slab", "gx"), "gy", None, None),
        P(("slab", "gx"), "gy", None),
    )
    out_specs = P(("slab", "gx"), "gy", None, None)
    return jax.shard_map(body, mesh=mesh, in_specs=in_specs, out_specs=out_specs, check_vma=False)
```

```python
import math

import jax
import jax.numpy as jnp
from jax import lax
from jax.experimental import pallas as pl
from jax.experimental.pallas import tpu as pltpu
from jax.sharding import PartitionSpec as P

BLOCK = 4
MESH = pl.DeviceIdType.MESH
F32 = jnp.float32
BF16 = jnp.bfloat16
X_ROWS = (slice(0, 1), slice(1, 7), slice(7, 8))


def kernel(
    count_gx,
    count_gy,
    x_hbm,
    taps_hbm,
    gain_hbm,
    wq_hbm,
    wk_hbm,
    wv_hbm,
    soft_hbm,
    codes_hbm,
    lens_hbm,
    hidden,
    attended,
    x_ref,
    taps_ref,
    gain_ref,
    wq_ref,
    wk_ref,
    wv_ref,
    soft_ref,
    codes_ref,
    lens_ref,
    framed,
    summed,
    rim_x,
    rim_y,
    rim_c,
    normed,
    near_x,
    near_y,
    query,
    key,
    value,
    key_x,
    value_x,
    key_y,
    value_y,
    acc,
    tot,
    send_sem,
    recv_sem,
    load_sem,
):
    operands = (
        (x_hbm, x_ref),
        (taps_hbm, taps_ref),
        (gain_hbm, gain_ref),
        (wk_hbm, wk_ref),
        (wv_hbm, wv_ref),
        (wq_hbm, wq_ref),
        (soft_hbm, soft_ref),
        (codes_hbm, codes_ref),
        (lens_hbm, lens_ref),
    )
    loads = [
        pltpu.make_async_copy(src, dst, load_sem.at[i]) for i, (src, dst) in enumerate(operands)
    ]
    for load in loads:
        load.start()
    gx = lax.axis_index("gx")
    gy = lax.axis_index("gy")
    has_x = (gx > 0, gx < count_gx - 1)
    has_y = (gy > 0, gy < count_gy - 1)
    step = (-1, 1)

    def target(dx, dy):
        return {"gx": gx + dx, "gy": gy + dy}

    def exists(dx, dy):
        conds = []
        if dx:
            conds.append(has_x[(dx + 1) // 2])
        if dy:
            conds.append(has_y[(dy + 1) // 2])
        return conds[0] if len(conds) == 1 else conds[0] & conds[1]

    around = [(dx, dy) for dx in (-1, 0, 1) for dy in (-1, 0, 1) if dx or dy]

    barrier = pltpu.get_barrier_semaphore()
    for dx, dy in around:

        @pl.when(exists(dx, dy))
        def _():
            pl.semaphore_signal(barrier, inc=1, device_id=target(dx, dy), device_id_type=MESH)

    span_x = 1 + has_x[0].astype(jnp.int32) + has_x[1].astype(jnp.int32)
    span_y = 1 + has_y[0].astype(jnp.int32) + has_y[1].astype(jnp.int32)
    pl.semaphore_wait(barrier, span_x * span_y - 1)

    def copy(src, dst, out_slot, in_slot, dx, dy):
        return pltpu.make_async_remote_copy(
            src_ref=src,
            dst_ref=dst,
            send_sem=send_sem.at[out_slot],
            recv_sem=recv_sem.at[in_slot],
            device_id=target(dx, dy),
            device_id_type=MESH,
        )

    rims = []
    landing = {}
    for side in (0, 1):
        other = 1 - side
        rims.append((step[side], 0, x_hbm.at[7 * side], rim_x.at[other], side, other))
        landing[side] = (step[side], 0, rim_x.at[side])
    for side in (0, 1):
        for side_y in (0, 1):
            at = 2 * side + side_y
            rims.append(
                (
                    step[side],
                    step[side_y],
                    x_hbm.at[7 * side, 7 * side_y],
                    rim_c.at[3 - at],
                    4 + at,
                    4 + 3 - at,
                )
            )
            landing[4 + at] = (step[side], step[side_y], rim_c.at[at])
    for side in (0, 1):
        other = 1 - side
        rims.append((0, step[side], x_hbm.at[:, 7 * side], rim_y.at[other], 2 + side, 2 + other))
        landing[2 + side] = (0, step[side], rim_y.at[side])

    early = (slice(0, 3), slice(1, 4))
    late = (3, 0)

    def face_y(side, at, slot=8):
        other = 1 - side
        return (
            0,
            step[side],
            normed.at[4 * side + at],
            near_y.at[other, at],
            8 + side,
            slot + other,
        )

    twin = 1 - gx % 2
    far = gx % 2
    twin_step = 1 - 2 * far
    far_x = gx - twin_step
    has_far = (far_x >= 0) & (far_x < count_gx)

    def face_x(rows):
        return pltpu.make_async_remote_copy(
            src_ref=normed.at[rows, far],
            dst_ref=near_x.at[rows],
            send_sem=send_sem.at[12],
            recv_sem=recv_sem.at[12],
            device_id={"gx": far_x, "gy": gy},
            device_id_type=MESH,
        )

    def twin_x(rows):
        return [
            pltpu.make_async_remote_copy(
                src_ref=src.at[rows, twin],
                dst_ref=dst.at[far, rows],
                send_sem=send_sem.at[13 + i],
                recv_sem=recv_sem.at[13 + i],
                device_id={"gx": gx + twin_step, "gy": gy},
                device_id_type=MESH,
            )
            for i, (src, dst) in enumerate(((key, key_x), (value, value_x)))
        ]

    def start_twin(part):
        for item in twin_x(X_ROWS[part]):
            item.start()

    def start_far(part):
        @pl.when(has_far)
        def _():
            face_x(X_ROWS[part]).start()

    for side in (0, 1):
        landing[8 + side] = (0, step[side], near_y.at[side, early[side]])
        landing[10 + side] = (0, step[side], near_y.at[side, late[side]])

    def start(item):
        dx, dy, src, dst, out_slot, in_slot = item

        @pl.when(exists(dx, dy))
        def _():
            copy(src, dst, out_slot, in_slot, dx, dy).start()

    def finish_send(item):
        dx, dy, src, dst, out_slot, in_slot = item
        copy(src, dst, out_slot, in_slot, dx, dy).wait_send()

    def arrive(slots, landed, absent=None):
        dx, dy, _ = landing[slots[0]]

        @pl.when(exists(dx, dy))
        def _():
            for slot in slots:
                buffer = landing[slot][2]
                copy(buffer, buffer, slot, slot, dx, dy).wait_recv()
            landed()

        if absent is not None:

            @pl.when(jnp.logical_not(exists(dx, dy)))
            def _():
                absent()

    for item in rims:
        start(item)

    for load in loads[:3]:
        load.wait()

    for at in (0, 9):
        framed[at] = jnp.zeros((10, 8, 512), F32)
        framed[:, at] = jnp.zeros((10, 8, 512), F32)

    @pl.loop(0, 8)
    def _(x):
        framed[1:9, x + 1] = x_ref[x].astype(F32)

    def add_taps(pieces, lanes):
        sums = [None, None, None]
        for a, b, piece in pieces:
            for c in range(3):
                tap = 9 * a + 3 * b + c
                coefficient = taps_ref[tap : tap + 1, lanes]
                if piece.ndim == 3:
                    coefficient = coefficient.reshape(1, 1, 128)
                term = piece * coefficient
                sums[c] = term if sums[c] is None else sums[c] + term
        axis = sums[0].ndim - 2
        depth_at = lax.broadcasted_iota(jnp.int32, sums[0].shape, axis)
        low = jnp.where(depth_at > 0, pltpu.roll(sums[0], 1, axis), 0.0)
        high = jnp.where(depth_at < 7, pltpu.roll(sums[2], 7, axis), 0.0)
        return sums[1] + low + high

    groups = [slice(128 * group, 128 * group + 128) for group in range(4)]

    @pl.loop(0, 8)
    def _(y):
        for lanes in groups:
            pieces = [
                (a, b, framed[y + b, a : a + 8, :, lanes]) for a in range(3) for b in range(3)
            ]
            own = framed[y + 1, 1:9, :, lanes]
            summed[y, :, :, lanes] = own + add_taps(pieces, lanes)

    for side in (0, 1):

        def landed(side=side):
            framed[1:9, 9 * side] = rim_x[side].astype(F32)
            for lanes in groups:
                pieces = [
                    (2 * side, b, framed[b : b + 8, 9 * side, :, lanes]) for b in range(3)
                ]
                before = summed[:, 7 * side, :, lanes]
                summed[:, 7 * side, :, lanes] = before + add_taps(pieces, lanes)

        arrive((side,), landed)

    half_at = lax.broadcasted_iota(jnp.int32, (4, 8, 512), 1) < 4
    gain = gain_ref[...].reshape(1, 1, 512)

    def finish_row(y):
        rows = summed[y].astype(BF16).astype(F32)
        pairs = rows.reshape(4, 2, 8, 512)
        even, odd = pairs[:, 0], pairs[:, 1]
        lower = jnp.where(half_at, even, pltpu.roll(odd, 4, 1))
        upper = jnp.where(half_at, pltpu.roll(even, 4, 1), odd)
        for bz, part in ((0, lower), (1, upper)):
            scale = lax.rsqrt(jnp.mean(part * part, axis=-1, keepdims=True) + 1e-05)
            unit = (part * scale * gain).reshape(2, 16, 512).astype(BF16)
            part = part.reshape(2, 16, 512).astype(BF16)
            for bx in (0, 1):
                hidden[y, bx, bz] = part[bx]
                normed[y, bx, bz] = unit[bx]

    @pl.loop(0, 3)
    def _(i):
        finish_row(1 + i)
        start(face_y(0, 1 + i))
        finish_row(6 - i)
        start(face_y(1, 2 - i))

    start_far(1)

    for load in loads[3:6]:
        load.wait()
    row = lax.broadcasted_iota(jnp.int32, (256, 256), 0) // 64
    column = lax.broadcasted_iota(jnp.int32, (256, 256), 1) // 64
    same_head = (row == column).astype(F32).astype(BF16)
    head_at = lax.broadcasted_iota(jnp.int32, (64, 256), 1) // 64
    head_of = lax.broadcasted_iota(jnp.int32, (16, 256), 1) // 64

    def units(raw):
        squares = (raw * raw).astype(BF16)
        sums = jnp.dot(squares, same_head, preferred_element_type=F32)
        return raw * lax.rsqrt(sums + 1e-06)

    def project(tokens, w_ref, quad):
        lanes = slice(256 * quad, 256 * quad + 256)
        return jnp.dot(tokens, w_ref[:, lanes], preferred_element_type=F32)

    def gather(parts):
        return jnp.concatenate([part[...].reshape(-1, 512) for part in parts], axis=0)

    def scatter(parts, lanes, values):
        at = 0
        for part in parts:
            shape = part.shape[:-1] + (256,)
            extent = math.prod(part.shape[:-1])
            part[..., lanes] = values[at : at + extent].reshape(shape)
            at += extent

    def keys_values(src, key_dst, value_dst):
        tokens = gather(src)
        for quad in (0, 1):
            lanes = slice(256 * quad, 256 * quad + 256)
            scatter(key_dst, lanes, units(project(tokens, wk_ref, quad)).astype(BF16))
            scatter(value_dst, lanes, project(tokens, wv_ref, quad).astype(BF16))

    def own_rows(spans):
        src = [normed.at[span] for span in spans]
        rows = [y for span in spans for y in range(span.start, span.stop)]
        tokens = gather(src)
        for quad in (0, 1):
            unit = units(project(tokens, wq_ref, quad)).reshape(len(rows), 2, 2, 16, 256)
            for i, y in enumerate(rows):
                by, yi = y // 4, y % 4
                for bx in (0, 1):
                    for bz in (0, 1):
                        for j in range(4):
                            kept = jnp.where(head_of == j, unit[i, bx, bz], 0.0)
                            at = 64 * j + 16 * yi
                            query[bx, by, bz, quad, at : at + 16] = kept.astype(BF16)
        keys_values(src, [key.at[s] for s in spans], [value.at[s] for s in spans])

    own_rows([slice(1, 4), slice(4, 7)])
    start_twin(1)

    def fill(index, ref):
        def landed():
            framed[index] = ref[...].astype(F32)

        return landed

    for side_y in (0, 1):
        at = 9 * side_y
        for side in (0, 1):
            slot = 2 * side + side_y
            arrive((4 + slot,), fill((at, 9 * side), rim_c.at[slot]))
        arrive((2 + side_y,), fill((at, slice(1, 9)), rim_y.at[side_y]))
        y = 7 * side_y
        for lanes in groups:
            pieces = [(a, 2 * side_y, framed[at, a : a + 8, :, lanes]) for a in range(3)]
            summed[y, :, :, lanes] = summed[y, :, :, lanes] + add_taps(pieces, lanes)
        finish_row(y)
        start(face_y(side_y, 3 * side_y, 10))
        start_far(2 * side_y)

    own_rows([slice(0, 1), slice(7, 8)])
    start_twin(0)
    start_twin(2)

    for load in loads[6:]:
        load.wait()
    log2e = math.log2(math.e)
    slots = codes_ref.shape[3]

    def attend(bx, by, bz, near):
        extent = 64 * len(near)
        slot_at = lax.broadcasted_iota(jnp.int32, (1, extent), 1) // 64
        named = jnp.full((1, extent), -2, jnp.int32)
        for j, (code, _, _) in enumerate(near):
            named = jnp.where(slot_at == j, code, named)
        mask = jnp.zeros((1, extent), F32)
        length = lens_ref[bx, by, bz]
        for s in range(slots):
            code = jnp.where(s < length, codes_ref[bx, by, bz, s], -1)
            mask = jnp.where(named == code, 1.0, mask)
        outs, sums = [], []
        for quad in (0, 1):
            lanes = slice(256 * quad, 256 * quad + 256)
            keys = jnp.concatenate([k[..., lanes].reshape(64, 256) for _, k, _ in near], axis=0)
            values = jnp.concatenate([v[..., lanes].reshape(64, 256) for _, _, v in near], axis=0)
            score = lax.dot_general(
                query[bx, by, bz, quad],
                keys,
                (((1,), (1,)), ((), ())),
                preferred_element_type=F32,
            )
            weights, totals = [], []
            for j in range(4):
                factor = soft_ref[4 * quad + j] * log2e
                weight = jnp.exp2(score[64 * j : 64 * j + 64] * factor) * mask
                totals.append(jnp.sum(weight, axis=-1, keepdims=True))
                weights.append(weight.astype(BF16))
            mixed = jnp.dot(
                jnp.concatenate(weights, axis=0), values, preferred_element_type=F32
            )
            out = mixed[0:64]
            total = jnp.broadcast_to(totals[0], (64, 256))
            for j in range(1, 4):
                out = jnp.where(head_at == j, mixed[64 * j : 64 * j + 64], out)
                total = jnp.where(head_at == j, totals[j], total)
            outs.append(out)
            sums.append(total)
        return outs, sums

    def attend_own(bx, by, bz):
        own, beside = pl.ds(4 * by, 4), pl.ds(4 - 4 * by, 4)
        near = [
            (6 * bz, key.at[own, bx, 0], value.at[own, bx, 0]),
            (5 * (1 - bz), key.at[own, bx, 1], value.at[own, bx, 1]),
            (1 + bx, key.at[own, 1 - bx, bz], value.at[own, 1 - bx, bz]),
            (3 + by, key.at[beside, bx, bz], value.at[beside, bx, bz]),
        ]
        outs, sums = attend(bx, by, bz, near)
        for quad in (0, 1):
            lanes = slice(256 * quad, 256 * quad + 256)
            acc[bx, by, bz, :, lanes] = outs[quad]
            tot[bx, by, bz, :, lanes] = sums[quad]

    for by in (0, 1):
        for bx in (0, 1):
            for bz in (0, 1):
                attend_own(bx, by, bz)

    def clear(*refs):
        def absent():
            for ref in refs:
                ref[...] = jnp.zeros(ref.shape, BF16)

        return absent

    @pl.when(has_far)
    def _():
        face_x(slice(0, 8)).wait_recv()
        keys_values([near_x], [key_x.at[far]], [value_x.at[far]])

    @pl.when(jnp.logical_not(has_far))
    def _():
        clear(key_x.at[far], value_x.at[far])()

    for side in (0, 1):
        span = early[side]
        arrive(
            (8 + side,),
            lambda side=side, span=span: keys_values(
                [near_y.at[side, span]], [key_y.at[side, span]], [value_y.at[side, span]]
            ),
            clear(key_y.at[side, span], value_y.at[side, span]),
        )
    for side in (0, 1):
        arrive((10 + side,), lambda: None, clear(near_y.at[side, late[side]]))
    keys_values(
        [near_y.at[side, late[side]] for side in (0, 1)],
        [key_y.at[side, late[side]] for side in (0, 1)],
        [value_y.at[side, late[side]] for side in (0, 1)],
    )

    for item in twin_x(slice(0, 8)):
        item.wait_recv()

    in_x = [has.astype(jnp.int32) for has in has_x]
    in_y = [has.astype(jnp.int32) for has in has_y]

    def attend_near(bx, by, bz):
        rows = pl.ds(4 * by, 4)
        near = [
            (
                jnp.where(in_x[bx] > 0, 2 - bx, -2),
                key_x.at[bx, rows, bz],
                value_x.at[bx, rows, bz],
            ),
            (
                jnp.where(in_y[by] > 0, 4 - by, -2),
                key_y.at[by, :, bx, bz],
                value_y.at[by, :, bx, bz],
            ),
        ]
        outs, sums = attend(bx, by, bz, near)
        for quad in (0, 1):
            lanes = slice(256 * quad, 256 * quad + 256)
            result = (acc[bx, by, bz, :, lanes] + outs[quad]) / (
                tot[bx, by, bz, :, lanes] + sums[quad]
            )
            attended[rows, bx, bz, :, lanes] = result.reshape(4, 16, 256).astype(BF16)

    for by in (0, 1):
        for bx in (0, 1):
            for bz in (0, 1):
                attend_near(bx, by, bz)
        rows = pl.ds(4 * by, 4)

    for item in twin_x(slice(0, 8)):
        item.wait_send()

    @pl.when(has_far)
    def _():
        face_x(slice(0, 8)).wait_send()

    for side in (0, 1):

        @pl.when(has_x[side])
        def _():
            finish_send(rims[side])
            for side_y in (0, 1):

                @pl.when(has_y[side_y])
                def _():
                    finish_send(rims[2 + 2 * side + side_y])

        @pl.when(has_y[side])
        def _():
            finish_send(rims[6 + side])
            rows = pl.ds(4 * side, 4)
            finish_send((0, step[side], normed.at[rows], near_y.at[side], 8 + side, 8 + side))


def finish(hidden, attended, wf_ref, out_hbm, out_ref, store_sem):
    stores = []
    for by in (0, 1):
        rows = pl.ds(4 * by, 4)
        update = jnp.dot(
            attended[rows].reshape(256, 512), wf_ref[...], preferred_element_type=F32
        )
        mixed = hidden[rows].reshape(256, 512).astype(F32) + update
        mixed = mixed.reshape(4, 2, 2, 2, 8, 512)
        lower = mixed[:, :, 0].reshape(16, 8, 512)
        upper = mixed[:, :, 1].reshape(16, 8, 512)
        split = lax.broadcasted_iota(jnp.int32, (16, 8, 512), 1) < 4
        even = jnp.where(split, lower, pltpu.roll(upper, 4, 1)).astype(BF16)
        odd = jnp.where(split, pltpu.roll(lower, 4, 1), upper).astype(BF16)
        for yi in range(4):
            for pair in range(4):
                out_ref[2 * pair, 4 * by + yi] = even[4 * yi + pair]
                out_ref[2 * pair + 1, 4 * by + yi] = odd[4 * yi + pair]
        store = pltpu.make_async_copy(out_ref.at[:, rows], out_hbm.at[:, rows], store_sem.at[by])
        store.start()
        stores.append(store)
    for store in stores:
        store.wait()


def solution(mesh):
    count_gx = mesh.shape["gx"]
    count_gy = mesh.shape["gy"]

    def body(x, taps, gain, wq, wk, wv, wf, soft, codes, lens):
        hbm = pl.BlockSpec(memory_space=pltpu.HBM)

        def run(*refs):
            kernel(count_gx, count_gy, *refs)

        x, taps, gain, wq, wk, wv, soft, codes, lens = (
            pltpu.with_memory_space_constraint(a, pltpu.HBM)
            for a in (x, taps, gain, wq, wk, wv, soft, codes, lens)
        )
        hidden, attended = pl.pallas_call(
            run,
            out_shape=[pltpu.VMEM((8, 2, 2, 16, 512), BF16)] * 2,
            in_specs=[hbm] * 9,
            out_specs=[pl.BlockSpec(memory_space=pltpu.VMEM)] * 2,
            scratch_shapes=[pltpu.VMEM(a.shape, a.dtype) for a in (x, taps, gain, wq, wk, wv)]
            + [pltpu.SMEM(a.shape, a.dtype) for a in (soft, codes, lens)]
            + [
                pltpu.VMEM((10, 10, 8, 512), F32),
                pltpu.VMEM((8, 8, 8, 512), F32),
                pltpu.VMEM((2, 8, 8, 512), BF16),
                pltpu.VMEM((2, 8, 8, 512), BF16),
                pltpu.VMEM((4, 8, 512), BF16),
                pltpu.VMEM((8, 2, 2, 16, 512), BF16),
                pltpu.VMEM((8, 2, 16, 512), BF16),
                pltpu.VMEM((2, 4, 2, 2, 16, 512), BF16),
                pltpu.VMEM((2, 2, 2, 2, 256, 256), BF16),
                pltpu.VMEM((8, 2, 2, 16, 512), BF16),
                pltpu.VMEM((8, 2, 2, 16, 512), BF16),
                pltpu.VMEM((2, 8, 2, 16, 512), BF16),
                pltpu.VMEM((2, 8, 2, 16, 512), BF16),
                pltpu.VMEM((2, 4, 2, 2, 16, 512), BF16),
                pltpu.VMEM((2, 4, 2, 2, 16, 512), BF16),
            ]
            + [pltpu.VMEM((2, 2, 2, 64, 512), F32)] * 2
            + [pltpu.SemaphoreType.DMA((count,)) for count in (15, 15, 9)],
            compiler_params=pltpu.CompilerParams(
                collective_id=0, has_side_effects=True, vmem_limit_bytes=32 * 1024 * 1024
            ),
            cost_estimate=pl.CostEstimate(
                flops=4 * 10**9, bytes_accessed=4 * 10**6, transcendentals=2 * 10**6
            ),
        )(x, taps, gain, wq, wk, wv, soft, codes, lens)
        vmem = pl.BlockSpec(memory_space=pltpu.VMEM)
        return pl.pallas_call(
            finish,
            out_shape=jax.ShapeDtypeStruct(x.shape, BF16),
            in_specs=[vmem, vmem, vmem],
            out_specs=hbm,
            scratch_shapes=[pltpu.VMEM(x.shape, BF16), pltpu.SemaphoreType.DMA((2,))],
            compiler_params=pltpu.CompilerParams(vmem_limit_bytes=8 * 1024 * 1024),
        )(hidden, attended, wf)

    in_specs = (
        P(("slab", "gx"), "gy", None, None),
        P(),
        P(),
        P(),
        P(),
        P(),
        P(),
        P(),
        P(("slab", "gx"), "gy", None, None),
        P(("slab", "gx"), "gy", None),
    )
    out_specs = P(("slab", "gx"), "gy", None, None)
    return jax.shard_map(body, mesh=mesh, in_specs=in_specs, out_specs=out_specs, check_vma=False)
```

```python
import math

import jax
import jax.numpy as jnp
from jax import lax
from jax.experimental import pallas as pl
from jax.experimental.pallas import tpu as pltpu
from jax.sharding import PartitionSpec as P

BLOCK = 4
MESH = pl.DeviceIdType.MESH
F32 = jnp.float32
BF16 = jnp.bfloat16
LOG2E = math.log2(math.e)
X_ROWS = (slice(0, 1), slice(1, 7), slice(7, 8))


def kernel(
    count_gx,
    count_gy,
    x_hbm,
    taps_hbm,
    gain_hbm,
    wq_hbm,
    wk_hbm,
    wv_hbm,
    soft_hbm,
    codes_hbm,
    lens_hbm,
    hidden,
    attended,
    x_ref,
    taps_ref,
    gain_ref,
    wq_ref,
    wk_ref,
    wv_ref,
    soft_ref,
    codes_ref,
    lens_ref,
    framed,
    summed,
    rim_x,
    rim_y,
    rim_c,
    normed,
    near_x,
    near_y,
    query,
    key,
    value,
    key_x,
    value_x,
    key_y,
    value_y,
    acc,
    tot,
    send_sem,
    recv_sem,
    load_sem,
):
    operands = (
        (x_hbm, x_ref),
        (taps_hbm, taps_ref),
        (gain_hbm, gain_ref),
        (wk_hbm, wk_ref),
        (wv_hbm, wv_ref),
        (wq_hbm, wq_ref),
        (soft_hbm, soft_ref),
        (codes_hbm, codes_ref),
        (lens_hbm, lens_ref),
    )
    loads = [
        pltpu.make_async_copy(src, dst, load_sem.at[i]) for i, (src, dst) in enumerate(operands)
    ]
    gx = lax.axis_index("gx")
    gy = lax.axis_index("gy")
    has_x = (gx > 0, gx < count_gx - 1)
    has_y = (gy > 0, gy < count_gy - 1)
    step = (-1, 1)

    def target(dx, dy):
        return {"gx": gx + dx, "gy": gy + dy}

    def exists(dx, dy):
        conds = []
        if dx:
            conds.append(has_x[(dx + 1) // 2])
        if dy:
            conds.append(has_y[(dy + 1) // 2])
        return conds[0] if len(conds) == 1 else conds[0] & conds[1]

    around = [(-1, 0), (1, 0), (0, -1), (0, 1)]

    barrier = pltpu.get_barrier_semaphore()
    for dx, dy in around:

        @pl.when(exists(dx, dy))
        def _():
            pl.semaphore_signal(barrier, inc=1, device_id=target(dx, dy), device_id_type=MESH)

    for load in loads[:3]:
        load.start()
    pl.semaphore_wait(barrier, sum(has.astype(jnp.int32) for has in has_x + has_y))

    def copy(src, dst, out_slot, in_slot, dx, dy):
        return pltpu.make_async_remote_copy(
            src_ref=src,
            dst_ref=dst,
            send_sem=send_sem.at[out_slot],
            recv_sem=recv_sem.at[in_slot],
            device_id=target(dx, dy),
            device_id_type=MESH,
        )

    rims = []
    landing = {}
    for side in (0, 1):
        other = 1 - side
        rims.append((step[side], 0, x_hbm.at[7 * side], rim_x.at[other], side, other))
        landing[side] = (step[side], 0, rim_x.at[side])
    for side in (0, 1):
        for side_y in (0, 1):
            at = 2 * side + side_y
            rims.append(
                (
                    0,
                    step[side_y],
                    rim_x.at[side, 7 * side_y],
                    rim_c.at[2 * side + 1 - side_y],
                    4 + at,
                    4 + 2 * side + 1 - side_y,
                )
            )
            landing[4 + at] = (step[side], step[side_y], rim_c.at[at])
    for side in (0, 1):
        other = 1 - side
        rims.append((0, step[side], x_hbm.at[:, 7 * side], rim_y.at[other], 2 + side, 2 + other))
        landing[2 + side] = (0, step[side], rim_y.at[side])

    early = (slice(0, 3), slice(1, 4))
    late = (3, 0)

    def face_y(side, at, slot=8):
        other = 1 - side
        return (
            0,
            step[side],
            normed.at[4 * side + at],
            near_y.at[other, at],
            8 + side,
            slot + other,
        )

    twin = 1 - gx % 2
    far = gx % 2
    twin_step = 1 - 2 * far
    far_x = gx - twin_step
    has_far = (far_x >= 0) & (far_x < count_gx)

    def face_x(rows):
        return pltpu.make_async_remote_copy(
            src_ref=normed.at[rows, far],
            dst_ref=near_x.at[rows],
            send_sem=send_sem.at[12],
            recv_sem=recv_sem.at[12],
            device_id={"gx": far_x, "gy": gy},
            device_id_type=MESH,
        )

    def twin_x(rows):
        return [
            pltpu.make_async_remote_copy(
                src_ref=src.at[rows, twin],
                dst_ref=dst.at[far, rows],
                send_sem=send_sem.at[13 + i],
                recv_sem=recv_sem.at[13 + i],
                device_id={"gx": gx + twin_step, "gy": gy},
                device_id_type=MESH,
            )
            for i, (src, dst) in enumerate(((key, key_x), (value, value_x)))
        ]

    def start_twin(part):
        for item in twin_x(X_ROWS[part]):
            item.start()

    def start_far(part):
        @pl.when(has_far)
        def _():
            face_x(X_ROWS[part]).start()

    for side in (0, 1):
        landing[8 + side] = (0, step[side], near_y.at[side, early[side]])
        landing[10 + side] = (0, step[side], near_y.at[side, late[side]])

    def start(item):
        dx, dy, src, dst, out_slot, in_slot = item

        @pl.when(exists(dx, dy))
        def _():
            copy(src, dst, out_slot, in_slot, dx, dy).start()

    def finish_send(item):
        dx, dy, src, dst, out_slot, in_slot = item
        copy(src, dst, out_slot, in_slot, dx, dy).wait_send()

    def arrive(slots, landed, absent=None):
        dx, dy, _ = landing[slots[0]]

        @pl.when(exists(dx, dy))
        def _():
            for slot in slots:
                buffer = landing[slot][2]
                copy(buffer, buffer, slot, slot, dx, dy).wait_recv()
            landed()

        if absent is not None:

            @pl.when(jnp.logical_not(exists(dx, dy)))
            def _():
                absent()

    for item in rims[6:] + rims[:2]:
        start(item)
    for load in loads[3:]:
        load.start()

    for load in loads[:3]:
        load.wait()

    for at in (0, 9):
        framed[at] = jnp.zeros((10, 8, 512), F32)
        framed[:, at] = jnp.zeros((10, 8, 512), F32)

    @pl.loop(0, 8)
    def _(x):
        framed[1:9, x + 1] = x_ref[x].astype(F32)

    def add_taps(pieces, lanes):
        sums = [None, None, None]
        for a, b, piece in pieces:
            for c in range(3):
                tap = 9 * a + 3 * b + c
                coefficient = taps_ref[tap : tap + 1, lanes]
                if piece.ndim == 3:
                    coefficient = coefficient.reshape(1, 1, 128)
                term = piece * coefficient
                sums[c] = term if sums[c] is None else sums[c] + term
        axis = sums[0].ndim - 2
        depth_at = lax.broadcasted_iota(jnp.int32, sums[0].shape, axis)
        low = jnp.where(depth_at > 0, pltpu.roll(sums[0], 1, axis), 0.0)
        high = jnp.where(depth_at < 7, pltpu.roll(sums[2], 7, axis), 0.0)
        return sums[1] + low + high

    groups = [slice(128 * group, 128 * group + 128) for group in range(4)]

    half_at = lax.broadcasted_iota(jnp.int32, (4, 8, 512), 1) < 4
    gain = gain_ref[...].reshape(1, 1, 512)

    def finish_row(y):
        rows = summed[y].astype(BF16).astype(F32)
        pairs = rows.reshape(4, 2, 8, 512)
        even, odd = pairs[:, 0], pairs[:, 1]
        lower = jnp.where(half_at, even, pltpu.roll(odd, 4, 1))
        upper = jnp.where(half_at, pltpu.roll(even, 4, 1), odd)
        for bz, part in ((0, lower), (1, upper)):
            scale = lax.rsqrt(jnp.mean(part * part, axis=-1, keepdims=True) + 1e-05)
            unit = (part * scale * gain).reshape(2, 16, 512).astype(BF16)
            part = part.reshape(2, 16, 512).astype(BF16)
            for bx in (0, 1):
                hidden[y, bx, bz] = part[bx]
                normed[y, bx, bz] = unit[bx]

    def finish_half(y, h):
        rows = summed[y, pl.ds(4 * h, 4)].astype(BF16).astype(F32)
        pairs = rows.reshape(2, 2, 8, 512)
        even, odd = pairs[:, 0], pairs[:, 1]
        first = half_at[:2]
        lower = jnp.where(first, even, pltpu.roll(odd, 4, 1))
        upper = jnp.where(first, pltpu.roll(even, 4, 1), odd)
        for bz, part in ((0, lower), (1, upper)):
            scale = lax.rsqrt(jnp.mean(part * part, axis=-1, keepdims=True) + 1e-05)
            hidden[y, h, bz] = part.reshape(16, 512).astype(BF16)
            normed[y, h, bz] = (part * scale * gain).reshape(16, 512).astype(BF16)

    def convolve_half(h):
        @pl.loop(0, 3)
        def _(i):
            y = 1 + 2 * i
            for lanes in groups:
                pieces = []
                for a in range(3):
                    for b in range(3):
                        piece = framed[pl.ds(y + b, 2), pl.ds(4 * h + a, 4), :, lanes]
                        pieces.append((a, b, piece.reshape(8, 8, 128)))
                own = framed[pl.ds(y + 1, 2), pl.ds(4 * h + 1, 4), :, lanes]
                result = own + add_taps(pieces, lanes).reshape(2, 4, 8, 128)
                summed[pl.ds(y, 2), pl.ds(4 * h, 4), :, lanes] = result

    def convolve_ends():
        @pl.loop(0, 2)
        def _(i):
            y = 7 * i
            for lanes in groups:
                pieces = [
                    (a, b, framed[y + b, a : a + 8, :, lanes]) for a in range(3) for b in range(3)
                ]
                own = framed[y + 1, 1:9, :, lanes]
                summed[y, :, :, lanes] = own + add_taps(pieces, lanes)

    def add_rim(side, first, last):
        dx, dy, buffer = landing[side]
        copy(buffer, buffer, side, side, dx, dy).wait_recv()
        for item in rims[2 + 2 * side : 4 + 2 * side]:
            start(item)
        framed[1:9, 9 * side] = rim_x[side].astype(F32)
        for lanes in groups:
            pieces = [(2 * side, b, framed[first + b : last + b, 9 * side, :, lanes]) for b in range(3)]
            before = summed[first:last, 7 * side, :, lanes]
            summed[first:last, 7 * side, :, lanes] = before + add_taps(pieces, lanes)

    for h, first, last in ((twin, 1, 7), (far, 0, 8)):
        convolve_half(h)
        if first == 0:
            pl.when(has_far)(convolve_ends)
        for side in (0, 1):

            @pl.when((h == side) & has_x[side])
            def _():
                add_rim(side, first, last)

        for toward in (0, 1):
            other = 1 - toward

            @pl.loop(1 + 3 * toward, 4 + 3 * toward)
            def _(y):
                finish_half(y, h)

            rows = slice(1 + 3 * toward, 4 + 3 * toward)
            start(
                (
                    0,
                    step[toward],
                    normed.at[rows, h],
                    near_y.at[other, early[other], h],
                    8 + toward,
                    8 + other,
                )
            )
    start_far(1)

    @pl.when(jnp.logical_not(has_far))
    def _():
        convolve_ends()

    for load in loads[3:]:
        load.wait()
    row = lax.broadcasted_iota(jnp.int32, (256, 256), 0) // 64
    column = lax.broadcasted_iota(jnp.int32, (256, 256), 1) // 64
    same_head = (row == column).astype(F32).astype(BF16)
    head_at = lax.broadcasted_iota(jnp.int32, (64, 256), 1) // 64
    head_of = lax.broadcasted_iota(jnp.int32, (16, 256), 1) // 64
    heads = [(head_of == j).astype(F32).astype(BF16) for j in range(4)]
    lane_head = lax.broadcasted_iota(jnp.int32, (1, 256), 1) // 64
    factors = []
    for quad in (0, 1):
        factor = jnp.zeros((1, 256), F32)
        for j in range(4):
            factor = jnp.where(lane_head == j, soft_ref[4 * quad + j] * LOG2E, factor)
        factors.append(factor)

    def units(raw):
        squares = (raw * raw).astype(BF16)
        sums = jnp.dot(squares, same_head, preferred_element_type=F32)
        return raw * lax.rsqrt(sums + 1e-06)

    def project(tokens, w_ref, quad):
        lanes = slice(256 * quad, 256 * quad + 256)
        return jnp.dot(tokens, w_ref[:, lanes], preferred_element_type=F32)

    def gather(parts):
        return jnp.concatenate([part[...].reshape(-1, 512) for part in parts], axis=0)

    def scatter(parts, lanes, values):
        at = 0
        for part in parts:
            shape = part.shape[:-1] + (256,)
            extent = math.prod(part.shape[:-1])
            part[..., lanes] = values[at : at + extent].reshape(shape)
            at += extent

    def keys_values(src, key_dst, value_dst):
        tokens = gather(src)
        for quad in (0, 1):
            lanes = slice(256 * quad, 256 * quad + 256)
            scatter(key_dst, lanes, units(project(tokens, wk_ref, quad)).astype(BF16))
            scatter(value_dst, lanes, project(tokens, wv_ref, quad).astype(BF16))

    def own_rows(spans):
        src = [normed.at[span] for span in spans]
        rows = [y for span in spans for y in range(span.start, span.stop)]
        tokens = gather(src)
        for quad in (0, 1):
            unit = units(project(tokens, wq_ref, quad)) * factors[quad]
            unit = unit.astype(BF16).reshape(len(rows), 2, 2, 16, 256)
            for i, y in enumerate(rows):
                by, yi = y // 4, y % 4
                for bx in (0, 1):
                    for bz in (0, 1):
                        for j in range(4):
                            kept = unit[i, bx, bz] * heads[j]
                            at = 64 * j + 16 * yi
                            query[bx, by, bz, quad, at : at + 16] = kept
        keys_values(src, [key.at[s] for s in spans], [value.at[s] for s in spans])


    own_rows([slice(1, 4), slice(4, 7)])
    start_twin(1)

    def fill(index, ref):
        def landed():
            framed[index] = ref[...].astype(F32)

        return landed

    for side_y in (0, 1):
        at = 9 * side_y
        for side in (0, 1):
            slot = 2 * side + side_y
            arrive((4 + slot,), fill((at, 9 * side), rim_c.at[slot]))
        arrive((2 + side_y,), fill((at, slice(1, 9)), rim_y.at[side_y]))
        y = 7 * side_y
        for lanes in groups:
            pieces = [(a, 2 * side_y, framed[at, a : a + 8, :, lanes]) for a in range(3)]
            summed[y, :, :, lanes] = summed[y, :, :, lanes] + add_taps(pieces, lanes)
        finish_row(y)
        start(face_y(side_y, 3 * side_y, 10))
        start_far(2 * side_y)

    own_rows([slice(0, 1), slice(7, 8)])
    start_twin(0)
    start_twin(2)

    slots = codes_ref.shape[3]

    def attend(bx, by, bz, near):
        extent = 64 * len(near)
        slot_at = lax.broadcasted_iota(jnp.int32, (1, extent), 1) // 64
        named = jnp.full((1, extent), -2, jnp.int32)
        for j, (code, _, _) in enumerate(near):
            named = jnp.where(slot_at == j, code, named)
        mask = jnp.zeros((1, extent), F32)
        length = lens_ref[bx, by, bz]
        for s in range(slots):
            code = jnp.where(s < length, codes_ref[bx, by, bz, s], -1)
            mask = jnp.where(named == code, 1.0, mask)
        outs, sums = [], []
        for quad in (0, 1):
            lanes = slice(256 * quad, 256 * quad + 256)
            keys = jnp.concatenate([k[..., lanes].reshape(64, 256) for _, k, _ in near], axis=0)
            values = jnp.concatenate([v[..., lanes].reshape(64, 256) for _, _, v in near], axis=0)
            score = lax.dot_general(
                query[bx, by, bz, quad],
                keys,
                (((1,), (1,)), ((), ())),
                preferred_element_type=F32,
            )
            weights, totals = [], []
            for j in range(4):
                weight = jnp.exp2(score[64 * j : 64 * j + 64]) * mask
                totals.append(jnp.sum(weight, axis=-1, keepdims=True))
                weights.append(weight.astype(BF16))
            mixed = jnp.dot(
                jnp.concatenate(weights, axis=0), values, preferred_element_type=F32
            )
            out = mixed[0:64]
            total = jnp.broadcast_to(totals[0], (64, 256))
            for j in range(1, 4):
                out = jnp.where(head_at == j, mixed[64 * j : 64 * j + 64], out)
                total = jnp.where(head_at == j, totals[j], total)
            outs.append(out)
            sums.append(total)
        return outs, sums

    def attend_own(bx, by, bz):
        own, beside = pl.ds(4 * by, 4), pl.ds(4 - 4 * by, 4)
        near = [
            (6 * bz, key.at[own, bx, 0], value.at[own, bx, 0]),
            (5 * (1 - bz), key.at[own, bx, 1], value.at[own, bx, 1]),
            (1 + bx, key.at[own, 1 - bx, bz], value.at[own, 1 - bx, bz]),
            (3 + by, key.at[beside, bx, bz], value.at[beside, bx, bz]),
        ]
        outs, sums = attend(bx, by, bz, near)
        for quad in (0, 1):
            lanes = slice(256 * quad, 256 * quad + 256)
            acc[bx, by, bz, :, lanes] = outs[quad]
            tot[bx, by, bz, :, lanes] = sums[quad]

    for by in (0, 1):
        for bx in (0, 1):
            for bz in (0, 1):
                attend_own(bx, by, bz)

    def clear(*refs):
        def absent():
            for ref in refs:
                ref[...] = jnp.zeros(ref.shape, BF16)

        return absent

    for side in (0, 1):
        span = early[side]
        arrive(
            (8 + side,),
            lambda side=side, span=span: keys_values(
                [near_y.at[side, span]], [key_y.at[side, span]], [value_y.at[side, span]]
            ),
            clear(key_y.at[side, span], value_y.at[side, span]),
        )
    @pl.when(has_far)
    def _():
        face_x(slice(0, 8)).wait_recv()
        keys_values([near_x], [key_x.at[far]], [value_x.at[far]])

    @pl.when(jnp.logical_not(has_far))
    def _():
        clear(key_x.at[far], value_x.at[far])()

    for side in (0, 1):
        arrive((10 + side,), lambda: None, clear(near_y.at[side, late[side]]))
    keys_values(
        [near_y.at[side, late[side]] for side in (0, 1)],
        [key_y.at[side, late[side]] for side in (0, 1)],
        [value_y.at[side, late[side]] for side in (0, 1)],
    )

    for item in twin_x(slice(0, 8)):
        item.wait_recv()

    in_x = [has.astype(jnp.int32) for has in has_x]
    in_y = [has.astype(jnp.int32) for has in has_y]

    def attend_near(bx, by, bz):
        rows = pl.ds(4 * by, 4)
        near = [
            (
                jnp.where(in_x[bx] > 0, 2 - bx, -2),
                key_x.at[bx, rows, bz],
                value_x.at[bx, rows, bz],
            ),
            (
                jnp.where(in_y[by] > 0, 4 - by, -2),
                key_y.at[by, :, bx, bz],
                value_y.at[by, :, bx, bz],
            ),
        ]
        outs, sums = attend(bx, by, bz, near)
        for quad in (0, 1):
            lanes = slice(256 * quad, 256 * quad + 256)
            result = (acc[bx, by, bz, :, lanes] + outs[quad]) / (
                tot[bx, by, bz, :, lanes] + sums[quad]
            )
            attended[rows, bx, bz, :, lanes] = result.reshape(4, 16, 256).astype(BF16)

    for by in (0, 1):
        for bx in (0, 1):
            for bz in (0, 1):
                attend_near(bx, by, bz)
        rows = pl.ds(4 * by, 4)

    for item in twin_x(slice(0, 8)):
        item.wait_send()

    @pl.when(has_far)
    def _():
        face_x(slice(0, 8)).wait_send()

    for side in (0, 1):

        @pl.when(has_x[side])
        def _():
            finish_send(rims[side])
            for side_y in (0, 1):

                @pl.when(has_y[side_y])
                def _():
                    finish_send(rims[2 + 2 * side + side_y])

        @pl.when(has_y[side])
        def _():
            finish_send(rims[6 + side])
            rows = pl.ds(4 * side, 4)
            finish_send((0, step[side], normed.at[rows], near_y.at[side], 8 + side, 8 + side))


def finish(hidden, attended, wf_ref, out_hbm, out_ref, store_sem):
    stores = []
    split = lax.broadcasted_iota(jnp.int32, (8, 8, 512), 1) < 4
    for part in range(4):
        rows = pl.ds(2 * part, 2)
        update = jnp.dot(
            attended[rows].reshape(128, 512), wf_ref[...], preferred_element_type=F32
        )
        mixed = hidden[rows].reshape(128, 512).astype(F32) + update
        mixed = mixed.reshape(2, 2, 2, 2, 8, 512)
        lower = mixed[:, :, 0].reshape(8, 8, 512)
        upper = mixed[:, :, 1].reshape(8, 8, 512)
        even = jnp.where(split, lower, pltpu.roll(upper, 4, 1)).astype(BF16)
        odd = jnp.where(split, pltpu.roll(lower, 4, 1), upper).astype(BF16)
        for yi in range(2):
            for pair in range(4):
                out_ref[2 * pair, 2 * part + yi] = even[4 * yi + pair]
                out_ref[2 * pair + 1, 2 * part + yi] = odd[4 * yi + pair]
        store = pltpu.make_async_copy(
            out_ref.at[:, rows], out_hbm.at[:, rows], store_sem.at[part]
        )
        store.start()
        stores.append(store)
    for store in stores:
        store.wait()


def solution(mesh):
    count_gx = mesh.shape["gx"]
    count_gy = mesh.shape["gy"]

    def body(x, taps, gain, wq, wk, wv, wf, soft, codes, lens):
        hbm = pl.BlockSpec(memory_space=pltpu.HBM)

        def run(*refs):
            kernel(count_gx, count_gy, *refs)

        x, taps, gain, wq, wk, wv, soft, codes, lens = (
            pltpu.with_memory_space_constraint(a, pltpu.HBM)
            for a in (x, taps, gain, wq, wk, wv, soft, codes, lens)
        )
        hidden, attended = pl.pallas_call(
            run,
            out_shape=[pltpu.VMEM((8, 2, 2, 16, 512), BF16)] * 2,
            in_specs=[hbm] * 9,
            out_specs=[pl.BlockSpec(memory_space=pltpu.VMEM)] * 2,
            scratch_shapes=[pltpu.VMEM(a.shape, a.dtype) for a in (x, taps, gain, wq, wk, wv)]
            + [pltpu.SMEM(a.shape, a.dtype) for a in (soft, codes, lens)]
            + [
                pltpu.VMEM((10, 10, 8, 512), F32),
                pltpu.VMEM((8, 8, 8, 512), F32),
                pltpu.VMEM((2, 8, 8, 512), BF16),
                pltpu.VMEM((2, 8, 8, 512), BF16),
                pltpu.VMEM((4, 8, 512), BF16),
                pltpu.VMEM((8, 2, 2, 16, 512), BF16),
                pltpu.VMEM((8, 2, 16, 512), BF16),
                pltpu.VMEM((2, 4, 2, 2, 16, 512), BF16),
                pltpu.VMEM((2, 2, 2, 2, 256, 256), BF16),
                pltpu.VMEM((8, 2, 2, 16, 512), BF16),
                pltpu.VMEM((8, 2, 2, 16, 512), BF16),
                pltpu.VMEM((2, 8, 2, 16, 512), BF16),
                pltpu.VMEM((2, 8, 2, 16, 512), BF16),
                pltpu.VMEM((2, 4, 2, 2, 16, 512), BF16),
                pltpu.VMEM((2, 4, 2, 2, 16, 512), BF16),
            ]
            + [pltpu.VMEM((2, 2, 2, 64, 512), F32)] * 2
            + [pltpu.SemaphoreType.DMA((count,)) for count in (15, 15, 9)],
            compiler_params=pltpu.CompilerParams(
                collective_id=0, has_side_effects=True, vmem_limit_bytes=32 * 1024 * 1024
            ),
            cost_estimate=pl.CostEstimate(
                flops=4 * 10**9, bytes_accessed=4 * 10**6, transcendentals=2 * 10**6
            ),
        )(x, taps, gain, wq, wk, wv, soft, codes, lens)
        vmem = pl.BlockSpec(memory_space=pltpu.VMEM)
        return pl.pallas_call(
            finish,
            out_shape=jax.ShapeDtypeStruct(x.shape, BF16),
            in_specs=[vmem, vmem, vmem],
            out_specs=hbm,
            scratch_shapes=[pltpu.VMEM(x.shape, BF16), pltpu.SemaphoreType.DMA((4,))],
            compiler_params=pltpu.CompilerParams(vmem_limit_bytes=8 * 1024 * 1024),
        )(hidden, attended, wf)

    in_specs = (
        P(("slab", "gx"), "gy", None, None),
        P(),
        P(),
        P(),
        P(),
        P(),
        P(),
        P(),
        P(("slab", "gx"), "gy", None, None),
        P(("slab", "gx"), "gy", None),
    )
    out_specs = P(("slab", "gx"), "gy", None, None)
    return jax.shard_map(body, mesh=mesh, in_specs=in_specs, out_specs=out_specs, check_vma=False)
```

```python
import math

import jax
import jax.numpy as jnp
from jax import lax
from jax.experimental import pallas as pl
from jax.experimental.pallas import tpu as pltpu
from jax.sharding import PartitionSpec as P

BLOCK = 4
MESH = pl.DeviceIdType.MESH
F32 = jnp.float32
BF16 = jnp.bfloat16
LOG2E = math.log2(math.e)
X_ROWS = (slice(0, 1), slice(1, 7), slice(7, 8))


def kernel(
    count_gx,
    count_gy,
    x_hbm,
    taps_hbm,
    gain_hbm,
    wq_hbm,
    wk_hbm,
    wv_hbm,
    soft_hbm,
    codes_hbm,
    lens_hbm,
    hidden,
    attended,
    x_ref,
    taps_ref,
    gain_ref,
    wq_ref,
    wk_ref,
    wv_ref,
    soft_ref,
    codes_ref,
    lens_ref,
    framed,
    summed,
    rim_x,
    rim_y,
    rim_c,
    normed,
    near_x,
    near_y,
    query,
    key,
    value,
    key_x,
    value_x,
    key_y,
    value_y,
    acc,
    tot,
    send_sem,
    recv_sem,
    load_sem,
):
    operands = (
        (x_hbm, x_ref),
        (taps_hbm, taps_ref),
        (gain_hbm, gain_ref),
        (wk_hbm, wk_ref),
        (wv_hbm, wv_ref),
        (wq_hbm, wq_ref),
        (soft_hbm, soft_ref),
        (codes_hbm, codes_ref),
        (lens_hbm, lens_ref),
    )
    loads = [
        pltpu.make_async_copy(src, dst, load_sem.at[i]) for i, (src, dst) in enumerate(operands)
    ]
    gx = lax.axis_index("gx")
    gy = lax.axis_index("gy")
    has_x = (gx > 0, gx < count_gx - 1)
    has_y = (gy > 0, gy < count_gy - 1)
    step = (-1, 1)

    def target(dx, dy):
        return {"gx": gx + dx, "gy": gy + dy}

    def exists(dx, dy):
        conds = []
        if dx:
            conds.append(has_x[(dx + 1) // 2])
        if dy:
            conds.append(has_y[(dy + 1) // 2])
        return conds[0] if len(conds) == 1 else conds[0] & conds[1]

    around = [(-1, 0), (1, 0), (0, -1), (0, 1)]

    barrier = pltpu.get_barrier_semaphore()
    for dx, dy in around:

        @pl.when(exists(dx, dy))
        def _():
            pl.semaphore_signal(barrier, inc=1, device_id=target(dx, dy), device_id_type=MESH)

    for load in loads[:3]:
        load.start()
    pl.semaphore_wait(barrier, sum(has.astype(jnp.int32) for has in has_x + has_y))

    def copy(src, dst, out_slot, in_slot, dx, dy):
        return pltpu.make_async_remote_copy(
            src_ref=src,
            dst_ref=dst,
            send_sem=send_sem.at[out_slot],
            recv_sem=recv_sem.at[in_slot],
            device_id=target(dx, dy),
            device_id_type=MESH,
        )

    rims = []
    landing = {}
    for side in (0, 1):
        other = 1 - side
        rims.append((step[side], 0, x_hbm.at[7 * side], rim_x.at[other], side, other))
        landing[side] = (step[side], 0, rim_x.at[side])
    for side in (0, 1):
        for side_y in (0, 1):
            at = 2 * side + side_y
            rims.append(
                (
                    0,
                    step[side_y],
                    rim_x.at[side, 7 * side_y],
                    rim_c.at[2 * side + 1 - side_y],
                    4 + at,
                    4 + 2 * side + 1 - side_y,
                )
            )
            landing[4 + at] = (step[side], step[side_y], rim_c.at[at])
    for side in (0, 1):
        other = 1 - side
        rims.append((0, step[side], x_hbm.at[:, 7 * side], rim_y.at[other], 2 + side, 2 + other))
        landing[2 + side] = (0, step[side], rim_y.at[side])

    early = (slice(0, 3), slice(1, 4))
    late = (3, 0)

    def face_y(side, at, slot=8):
        other = 1 - side
        return (
            0,
            step[side],
            normed.at[4 * side + at],
            near_y.at[other, at],
            8 + side,
            slot + other,
        )

    twin = 1 - gx % 2
    far = gx % 2
    twin_step = 1 - 2 * far
    far_x = gx - twin_step
    has_far = (far_x >= 0) & (far_x < count_gx)

    def face_x(rows):
        return pltpu.make_async_remote_copy(
            src_ref=normed.at[rows, far],
            dst_ref=near_x.at[rows],
            send_sem=send_sem.at[12],
            recv_sem=recv_sem.at[12],
            device_id={"gx": far_x, "gy": gy},
            device_id_type=MESH,
        )

    def twin_x(rows):
        return [
            pltpu.make_async_remote_copy(
                src_ref=src.at[rows, twin],
                dst_ref=dst.at[far, rows],
                send_sem=send_sem.at[13 + i],
                recv_sem=recv_sem.at[13 + i],
                device_id={"gx": gx + twin_step, "gy": gy},
                device_id_type=MESH,
            )
            for i, (src, dst) in enumerate(((key, key_x), (value, value_x)))
        ]

    def start_twin(part):
        for item in twin_x(X_ROWS[part]):
            item.start()

    def start_far(part):
        @pl.when(has_far)
        def _():
            face_x(X_ROWS[part]).start()

    for side in (0, 1):
        landing[8 + side] = (0, step[side], near_y.at[side, early[side]])
        landing[10 + side] = (0, step[side], near_y.at[side, late[side]])

    def start(item):
        dx, dy, src, dst, out_slot, in_slot = item

        @pl.when(exists(dx, dy))
        def _():
            copy(src, dst, out_slot, in_slot, dx, dy).start()

    def finish_send(item):
        dx, dy, src, dst, out_slot, in_slot = item
        copy(src, dst, out_slot, in_slot, dx, dy).wait_send()

    def arrive(slots, landed, absent=None):
        dx, dy, _ = landing[slots[0]]

        @pl.when(exists(dx, dy))
        def _():
            for slot in slots:
                buffer = landing[slot][2]
                copy(buffer, buffer, slot, slot, dx, dy).wait_recv()
            landed()

        if absent is not None:

            @pl.when(jnp.logical_not(exists(dx, dy)))
            def _():
                absent()

    for item in rims[:2] + rims[6:]:
        start(item)
    for load in loads[3:]:
        load.start()

    for load in loads[:3]:
        load.wait()

    for at in (0, 9):
        framed[at] = jnp.zeros((10, 8, 512), F32)
        framed[:, at] = jnp.zeros((10, 8, 512), F32)

    @pl.loop(0, 8)
    def _(x):
        framed[1:9, x + 1] = x_ref[x].astype(F32)

    def add_taps(pieces, lanes):
        sums = [None, None, None]
        for a, b, piece in pieces:
            for c in range(3):
                tap = 9 * a + 3 * b + c
                coefficient = taps_ref[tap : tap + 1, lanes]
                if piece.ndim == 3:
                    coefficient = coefficient.reshape(1, 1, 128)
                term = piece * coefficient
                sums[c] = term if sums[c] is None else sums[c] + term
        axis = sums[0].ndim - 2
        depth_at = lax.broadcasted_iota(jnp.int32, sums[0].shape, axis)
        low = jnp.where(depth_at > 0, pltpu.roll(sums[0], 1, axis), 0.0)
        high = jnp.where(depth_at < 7, pltpu.roll(sums[2], 7, axis), 0.0)
        return sums[1] + low + high

    groups = [slice(128 * group, 128 * group + 128) for group in range(4)]

    half_at = lax.broadcasted_iota(jnp.int32, (4, 8, 512), 1) < 4
    gain = gain_ref[...].reshape(1, 1, 512)

    def finish_row(y):
        rows = summed[y].astype(BF16).astype(F32)
        pairs = rows.reshape(4, 2, 8, 512)
        even, odd = pairs[:, 0], pairs[:, 1]
        lower = jnp.where(half_at, even, pltpu.roll(odd, 4, 1))
        upper = jnp.where(half_at, pltpu.roll(even, 4, 1), odd)
        for bz, part in ((0, lower), (1, upper)):
            scale = lax.rsqrt(jnp.mean(part * part, axis=-1, keepdims=True) + 1e-05)
            unit = (part * scale * gain).reshape(2, 16, 512).astype(BF16)
            part = part.reshape(2, 16, 512).astype(BF16)
            for bx in (0, 1):
                hidden[y, bx, bz] = part[bx]
                normed[y, bx, bz] = unit[bx]

    def finish_half(y, h):
        rows = summed[y, pl.ds(4 * h, 4)].astype(BF16).astype(F32)
        pairs = rows.reshape(2, 2, 8, 512)
        even, odd = pairs[:, 0], pairs[:, 1]
        first = half_at[:2]
        lower = jnp.where(first, even, pltpu.roll(odd, 4, 1))
        upper = jnp.where(first, pltpu.roll(even, 4, 1), odd)
        for bz, part in ((0, lower), (1, upper)):
            scale = lax.rsqrt(jnp.mean(part * part, axis=-1, keepdims=True) + 1e-05)
            hidden[y, h, bz] = part.reshape(16, 512).astype(BF16)
            normed[y, h, bz] = (part * scale * gain).reshape(16, 512).astype(BF16)

    def convolve_half(h):
        @pl.loop(0, 3)
        def _(i):
            y = 1 + 2 * i
            for lanes in groups:
                pieces = []
                for a in range(3):
                    for b in range(3):
                        piece = framed[pl.ds(y + b, 2), pl.ds(4 * h + a, 4), :, lanes]
                        pieces.append((a, b, piece.reshape(8, 8, 128)))
                own = framed[pl.ds(y + 1, 2), pl.ds(4 * h + 1, 4), :, lanes]
                result = own + add_taps(pieces, lanes).reshape(2, 4, 8, 128)
                summed[pl.ds(y, 2), pl.ds(4 * h, 4), :, lanes] = result

    def convolve_ends():
        @pl.loop(0, 2)
        def _(i):
            y = 7 * i
            for lanes in groups:
                pieces = [
                    (a, b, framed[y + b, a : a + 8, :, lanes]) for a in range(3) for b in range(3)
                ]
                own = framed[y + 1, 1:9, :, lanes]
                summed[y, :, :, lanes] = own + add_taps(pieces, lanes)

    def add_rim(side, first, last):
        dx, dy, buffer = landing[side]
        copy(buffer, buffer, side, side, dx, dy).wait_recv()
        for item in rims[2 + 2 * side : 4 + 2 * side]:
            start(item)
        framed[1:9, 9 * side] = rim_x[side].astype(F32)
        for lanes in groups:
            pieces = [(2 * side, b, framed[first + b : last + b, 9 * side, :, lanes]) for b in range(3)]
            before = summed[first:last, 7 * side, :, lanes]
            summed[first:last, 7 * side, :, lanes] = before + add_taps(pieces, lanes)

    for h, first, last in ((twin, 1, 7), (far, 0, 8)):
        convolve_half(h)
        if first == 0:
            pl.when(has_far)(convolve_ends)
        for side in (0, 1):

            @pl.when((h == side) & has_x[side])
            def _():
                add_rim(side, first, last)

        for toward in (0, 1):
            other = 1 - toward

            @pl.loop(1 + 3 * toward, 4 + 3 * toward)
            def _(y):
                finish_half(y, h)

            rows = slice(1 + 3 * toward, 4 + 3 * toward)
            start(
                (
                    0,
                    step[toward],
                    normed.at[rows, h],
                    near_y.at[other, early[other], h],
                    8 + toward,
                    8 + other,
                )
            )
    start_far(1)

    @pl.when(jnp.logical_not(has_far))
    def _():
        convolve_ends()

    for load in loads[3:]:
        load.wait()
    row = lax.broadcasted_iota(jnp.int32, (256, 256), 0) // 64
    column = lax.broadcasted_iota(jnp.int32, (256, 256), 1) // 64
    same_head = (row == column).astype(F32).astype(BF16)
    head_at = lax.broadcasted_iota(jnp.int32, (64, 256), 1) // 64
    head_of = lax.broadcasted_iota(jnp.int32, (16, 256), 1) // 64
    heads = [(head_of == j).astype(F32).astype(BF16) for j in range(4)]
    lane_head = lax.broadcasted_iota(jnp.int32, (1, 256), 1) // 64
    factors = []
    for quad in (0, 1):
        factor = jnp.zeros((1, 256), F32)
        for j in range(4):
            factor = jnp.where(lane_head == j, soft_ref[4 * quad + j] * LOG2E, factor)
        factors.append(factor)

    def units(raw):
        rounded = raw.astype(BF16)
        squares = rounded * rounded
        sums = jnp.dot(squares, same_head, preferred_element_type=F32)
        return raw * lax.rsqrt(sums + 1e-06)

    def project(tokens, w_ref, quad):
        lanes = slice(256 * quad, 256 * quad + 256)
        return jnp.dot(tokens, w_ref[:, lanes], preferred_element_type=F32)

    def gather(parts):
        return jnp.concatenate([part[...].reshape(-1, 512) for part in parts], axis=0)

    def scatter(parts, lanes, values):
        at = 0
        for part in parts:
            shape = part.shape[:-1] + (256,)
            extent = math.prod(part.shape[:-1])
            part[..., lanes] = values[at : at + extent].reshape(shape)
            at += extent

    def keys_values(src, key_dst, value_dst):
        tokens = gather(src)
        for quad in (0, 1):
            lanes = slice(256 * quad, 256 * quad + 256)
            scatter(key_dst, lanes, units(project(tokens, wk_ref, quad)).astype(BF16))
            scatter(value_dst, lanes, project(tokens, wv_ref, quad).astype(BF16))

    def own_rows(spans):
        src = [normed.at[span] for span in spans]
        rows = [y for span in spans for y in range(span.start, span.stop)]
        tokens = gather(src)
        for quad in (0, 1):
            unit = units(project(tokens, wq_ref, quad)) * factors[quad]
            unit = unit.astype(BF16).reshape(len(rows), 2, 2, 16, 256)
            for i, y in enumerate(rows):
                by, yi = y // 4, y % 4
                for bx in (0, 1):
                    for bz in (0, 1):
                        for j in range(4):
                            kept = unit[i, bx, bz] * heads[j]
                            at = 64 * j + 16 * yi
                            query[bx, by, bz, quad, at : at + 16] = kept
        keys_values(src, [key.at[s] for s in spans], [value.at[s] for s in spans])


    own_rows([slice(1, 4), slice(4, 7)])
    start_twin(1)

    def fill(index, ref):
        def landed():
            framed[index] = ref[...].astype(F32)

        return landed

    for side_y in (0, 1):
        at = 9 * side_y
        for side in (0, 1):
            slot = 2 * side + side_y
            arrive((4 + slot,), fill((at, 9 * side), rim_c.at[slot]))
        arrive((2 + side_y,), fill((at, slice(1, 9)), rim_y.at[side_y]))
        y = 7 * side_y
        for lanes in groups:
            pieces = [(a, 2 * side_y, framed[at, a : a + 8, :, lanes]) for a in range(3)]
            summed[y, :, :, lanes] = summed[y, :, :, lanes] + add_taps(pieces, lanes)
        finish_row(y)
        start(face_y(side_y, 3 * side_y, 10))
        start_far(2 * side_y)

    own_rows([slice(0, 1), slice(7, 8)])
    start_twin(0)
    start_twin(2)

    slots = codes_ref.shape[3]

    def attend(bx, by, bz, near):
        extent = 64 * len(near)
        slot_at = lax.broadcasted_iota(jnp.int32, (1, extent), 1) // 64
        named = jnp.full((1, extent), -2, jnp.int32)
        for j, (code, _, _) in enumerate(near):
            named = jnp.where(slot_at == j, code, named)
        mask = jnp.zeros((1, extent), F32)
        length = lens_ref[bx, by, bz]
        for s in range(slots):
            code = jnp.where(s < length, codes_ref[bx, by, bz, s], -1)
            mask = jnp.where(named == code, 1.0, mask)
        outs, sums = [], []
        for quad in (0, 1):
            lanes = slice(256 * quad, 256 * quad + 256)
            keys = jnp.concatenate([k[..., lanes].reshape(64, 256) for _, k, _ in near], axis=0)
            values = jnp.concatenate([v[..., lanes].reshape(64, 256) for _, _, v in near], axis=0)
            score = lax.dot_general(
                query[bx, by, bz, quad],
                keys,
                (((1,), (1,)), ((), ())),
                preferred_element_type=F32,
            )
            weights, totals = [], []
            for j in range(4):
                weight = jnp.exp2(score[64 * j : 64 * j + 64]) * mask
                totals.append(jnp.sum(weight, axis=-1, keepdims=True))
                weights.append(weight.astype(BF16))
            mixed = jnp.dot(
                jnp.concatenate(weights, axis=0), values, preferred_element_type=F32
            )
            out = mixed[0:64]
            total = jnp.broadcast_to(totals[0], (64, 256))
            for j in range(1, 4):
                out = jnp.where(head_at == j, mixed[64 * j : 64 * j + 64], out)
                total = jnp.where(head_at == j, totals[j], total)
            outs.append(out)
            sums.append(total)
        return outs, sums

    def attend_own(bx, by, bz):
        own, beside = pl.ds(4 * by, 4), pl.ds(4 - 4 * by, 4)
        near = [
            (6 * bz, key.at[own, bx, 0], value.at[own, bx, 0]),
            (5 * (1 - bz), key.at[own, bx, 1], value.at[own, bx, 1]),
            (1 + bx, key.at[own, 1 - bx, bz], value.at[own, 1 - bx, bz]),
            (3 + by, key.at[beside, bx, bz], value.at[beside, bx, bz]),
        ]
        outs, sums = attend(bx, by, bz, near)
        for quad in (0, 1):
            lanes = slice(256 * quad, 256 * quad + 256)
            acc[bx, by, bz, :, lanes] = outs[quad]
            tot[bx, by, bz, :, lanes] = sums[quad]

    for by in (0, 1):
        for bx in (0, 1):
            for bz in (0, 1):
                attend_own(bx, by, bz)

    def clear(*refs):
        def absent():
            for ref in refs:
                ref[...] = jnp.zeros(ref.shape, BF16)

        return absent

    for side in (0, 1):
        span = early[side]
        arrive(
            (8 + side,),
            lambda side=side, span=span: keys_values(
                [near_y.at[side, span]], [key_y.at[side, span]], [value_y.at[side, span]]
            ),
            clear(key_y.at[side, span], value_y.at[side, span]),
        )
    @pl.when(has_far)
    def _():
        face_x(slice(0, 8)).wait_recv()
        keys_values([near_x], [key_x.at[far]], [value_x.at[far]])

    @pl.when(jnp.logical_not(has_far))
    def _():
        clear(key_x.at[far], value_x.at[far])()

    for side in (0, 1):
        arrive((10 + side,), lambda: None, clear(near_y.at[side, late[side]]))
    keys_values(
        [near_y.at[side, late[side]] for side in (0, 1)],
        [key_y.at[side, late[side]] for side in (0, 1)],
        [value_y.at[side, late[side]] for side in (0, 1)],
    )

    for item in twin_x(slice(0, 8)):
        item.wait_recv()

    in_x = [has.astype(jnp.int32) for has in has_x]
    in_y = [has.astype(jnp.int32) for has in has_y]

    def attend_near(bx, by, bz):
        rows = pl.ds(4 * by, 4)
        near = [
            (
                jnp.where(in_x[bx] > 0, 2 - bx, -2),
                key_x.at[bx, rows, bz],
                value_x.at[bx, rows, bz],
            ),
            (
                jnp.where(in_y[by] > 0, 4 - by, -2),
                key_y.at[by, :, bx, bz],
                value_y.at[by, :, bx, bz],
            ),
        ]
        outs, sums = attend(bx, by, bz, near)
        for quad in (0, 1):
            lanes = slice(256 * quad, 256 * quad + 256)
            total = tot[bx, by, bz, :, lanes] + sums[quad]
            inverse = pl.reciprocal(total, approx=True)
            inverse = inverse * (2.0 - total * inverse)
            result = (acc[bx, by, bz, :, lanes] + outs[quad]) * inverse
            attended[rows, bx, bz, :, lanes] = result.reshape(4, 16, 256).astype(BF16)

    for by in (0, 1):
        for bx in (0, 1):
            for bz in (0, 1):
                attend_near(bx, by, bz)
        rows = pl.ds(4 * by, 4)

    for item in twin_x(slice(0, 8)):
        item.wait_send()

    @pl.when(has_far)
    def _():
        face_x(slice(0, 8)).wait_send()

    for side in (0, 1):

        @pl.when(has_x[side])
        def _():
            finish_send(rims[side])
            for side_y in (0, 1):

                @pl.when(has_y[side_y])
                def _():
                    finish_send(rims[2 + 2 * side + side_y])

        @pl.when(has_y[side])
        def _():
            finish_send(rims[6 + side])
            rows = pl.ds(4 * side, 4)
            finish_send((0, step[side], normed.at[rows], near_y.at[side], 8 + side, 8 + side))


def finish(hidden, attended, wf_ref, out_hbm, out_ref, store_sem):
    stores = []
    split = lax.broadcasted_iota(jnp.int32, (8, 8, 512), 1) < 4
    for part in range(4):
        rows = pl.ds(2 * part, 2)
        update = jnp.dot(
            attended[rows].reshape(128, 512), wf_ref[...], preferred_element_type=F32
        )
        mixed = hidden[rows].reshape(128, 512).astype(F32) + update
        mixed = mixed.reshape(2, 2, 2, 2, 8, 512)
        lower = mixed[:, :, 0].reshape(8, 8, 512)
        upper = mixed[:, :, 1].reshape(8, 8, 512)
        even = jnp.where(split, lower, pltpu.roll(upper, 4, 1)).astype(BF16)
        odd = jnp.where(split, pltpu.roll(lower, 4, 1), upper).astype(BF16)
        for yi in range(2):
            for pair in range(4):
                out_ref[2 * pair, 2 * part + yi] = even[4 * yi + pair]
                out_ref[2 * pair + 1, 2 * part + yi] = odd[4 * yi + pair]
        store = pltpu.make_async_copy(
            out_ref.at[:, rows], out_hbm.at[:, rows], store_sem.at[part]
        )
        store.start()
        stores.append(store)
    for store in stores:
        store.wait()


def solution(mesh):
    count_gx = mesh.shape["gx"]
    count_gy = mesh.shape["gy"]

    def body(x, taps, gain, wq, wk, wv, wf, soft, codes, lens):
        hbm = pl.BlockSpec(memory_space=pltpu.HBM)

        def run(*refs):
            kernel(count_gx, count_gy, *refs)

        x, taps, gain, wq, wk, wv, soft, codes, lens = (
            pltpu.with_memory_space_constraint(a, pltpu.HBM)
            for a in (x, taps, gain, wq, wk, wv, soft, codes, lens)
        )
        hidden, attended = pl.pallas_call(
            run,
            out_shape=[pltpu.VMEM((8, 2, 2, 16, 512), BF16)] * 2,
            in_specs=[hbm] * 9,
            out_specs=[pl.BlockSpec(memory_space=pltpu.VMEM)] * 2,
            scratch_shapes=[pltpu.VMEM(a.shape, a.dtype) for a in (x, taps, gain, wq, wk, wv)]
            + [pltpu.SMEM(a.shape, a.dtype) for a in (soft, codes, lens)]
            + [
                pltpu.VMEM((10, 10, 8, 512), F32),
                pltpu.VMEM((8, 8, 8, 512), F32),
                pltpu.VMEM((2, 8, 8, 512), BF16),
                pltpu.VMEM((2, 8, 8, 512), BF16),
                pltpu.VMEM((4, 8, 512), BF16),
                pltpu.VMEM((8, 2, 2, 16, 512), BF16),
                pltpu.VMEM((8, 2, 16, 512), BF16),
                pltpu.VMEM((2, 4, 2, 2, 16, 512), BF16),
                pltpu.VMEM((2, 2, 2, 2, 256, 256), BF16),
                pltpu.VMEM((8, 2, 2, 16, 512), BF16),
                pltpu.VMEM((8, 2, 2, 16, 512), BF16),
                pltpu.VMEM((2, 8, 2, 16, 512), BF16),
                pltpu.VMEM((2, 8, 2, 16, 512), BF16),
                pltpu.VMEM((2, 4, 2, 2, 16, 512), BF16),
                pltpu.VMEM((2, 4, 2, 2, 16, 512), BF16),
            ]
            + [pltpu.VMEM((2, 2, 2, 64, 512), F32)] * 2
            + [pltpu.SemaphoreType.DMA((count,)) for count in (15, 15, 9)],
            compiler_params=pltpu.CompilerParams(
                collective_id=0, has_side_effects=True, vmem_limit_bytes=32 * 1024 * 1024
            ),
            cost_estimate=pl.CostEstimate(
                flops=4 * 10**9, bytes_accessed=4 * 10**6, transcendentals=2 * 10**6
            ),
        )(x, taps, gain, wq, wk, wv, soft, codes, lens)
        vmem = pl.BlockSpec(memory_space=pltpu.VMEM)
        return pl.pallas_call(
            finish,
            out_shape=jax.ShapeDtypeStruct(x.shape, BF16),
            in_specs=[vmem, vmem, vmem],
            out_specs=hbm,
            scratch_shapes=[pltpu.VMEM(x.shape, BF16), pltpu.SemaphoreType.DMA((4,))],
            compiler_params=pltpu.CompilerParams(vmem_limit_bytes=8 * 1024 * 1024),
        )(hidden, attended, wf)

    in_specs = (
        P(("slab", "gx"), "gy", None, None),
        P(),
        P(),
        P(),
        P(),
        P(),
        P(),
        P(),
        P(("slab", "gx"), "gy", None, None),
        P(("slab", "gx"), "gy", None),
    )
    out_specs = P(("slab", "gx"), "gy", None, None)
    return jax.shard_map(body, mesh=mesh, in_specs=in_specs, out_specs=out_specs, check_vma=False)
```
